128 devices in a mesh: ctx: 32 (over z, x, core), head: 4 (over y).
Axes of the slice: x: 4, y: 4, z: 4, core: 2. Of those that a mesh axis runs over, the one named last changes fastest.
Arguments:
- queries: float32 [32768, 8, 256], P('ctx', 'head'), may hold values from -6 to 6
- keys: float32 [32768, 8, 256], P('ctx', 'head'), may hold values from -6 to 6
- values: float32 [32768, 8, 512], P('ctx', 'head'), may hold values from -6 to 6
- entry_gate_logit: float32 [8, 32768], P('head', 'ctx'), may hold values from -10 to 300
- forget_gate: float32 [8, 32768], P('head', 'ctx'), may hold values from 0 to 20
- out_weight: bfloat16 [4096, 4096], P('head'), may hold values from -0.09375 to 0.09375
Outputs:
- mixed: bfloat16 [32768, 4096], P('ctx', 'head')
The draws below stay inside these ranges and needn't reach their ends.
All inputs are finite; a program needn't handle non-finite values.
Results may differ from the reference program's by a relative error of at most 0.013.
Values may be sent and summed in bfloat16 or wider, within the bound.
A program may use at most 192 MiB of HBM per device.

```python
import jax
import jax.numpy as jnp
from jax import lax

D = 4096
H = 8
DK = 256
DV = 512
TOK_DEV = 1024
TOKENS = 32768
N_HEAD = 4


def draw_forget_gate(key, part):
    key = jax.random.fold_in(key, 11)
    parts = jax.random.split(key, 7)
    slow_count = H // 2
    order = jax.random.permutation(parts[0], H)
    sluggish_items = order < slow_count
    slow_rate = 0.3 / TOKENS * jax.random.uniform(parts[1], (H,), minval=0.3, maxval=1.0)
    fast_rate = jax.random.uniform(parts[2], (H,), minval=1.0 / 50.0, maxval=1.0 / 30.0)
    rate = jnp.where(sluggish_items, slow_rate, fast_rate)[:, None]
    shard = jax.random.uniform(parts[3], (H, TOKENS // TOK_DEV), minval=0.5, maxval=2.0)
    shard = jnp.repeat(shard, TOK_DEV, axis=1)
    noise = jnp.exp(0.5 * jnp.clip(jax.random.normal(parts[4], (H, TOKENS)), -3.0, 3.0))
    shrink_multiplier = rate * shard * noise
    spots = jax.random.randint(parts[5], (H, 2), 0, TOKENS)
    sequence_offset = jnp.arange(TOKENS)[None, None, :] == spots[:, :, None]
    spurt_span = jnp.any(sequence_offset, axis=1) & sluggish_items[:, None]
    retained_entries = jax.random.uniform(parts[6], (H, TOKENS), minval=0.5, maxval=0.8)
    shrink_multiplier = jnp.where(spurt_span, -jnp.log(retained_entries), shrink_multiplier)
    return (-shrink_multiplier - jnp.log(-jnp.expm1(-shrink_multiplier))).astype(jnp.float32)


def draw_entry_gate_logit(key, part):
    key = jax.random.fold_in(key, 23)
    parts = jax.random.split(key, 1)
    base = 2.0 * jnp.clip(jax.random.normal(parts[0], (H, TOKENS)), -5.0, 5.0)
    return base.astype(jnp.float32)


def shard_levels(rng, extent, shards, least, largest):
    loudness, own = 1.0, jax.random.fold_in(rng, 6)
    for axis_at, blocks in shards:
        heights = jnp.exp(jax.random.uniform(jax.random.fold_in(own, axis_at), (blocks,), jnp.float32, least / len(shards), largest / len(shards)))
        loudness = loudness * jnp.repeat(heights, extent[axis_at] // blocks).reshape([-1 if axis == axis_at else 1 for axis in range(len(extent))])
    return loudness


def scatter_about(stream_key, extent, scale, most, cuts=(), held_as=jnp.bfloat16):
    result = jax.random.normal(stream_key, extent, jnp.float32) * scale
    if len(cuts) > 0:
        result = shard_levels(stream_key, extent, cuts, -0.22, 0.18) * result
    return jnp.clip(result, min=-most, max=most).astype(held_as)


def setup_inputs(seed: int = 0) -> dict:
    streams_of = jax.random.split(jax.random.key(seed), 7)
    queries = scatter_about(streams_of[0], (TOKENS, H, DK), 1.0, 6.0, ((0, 32), (1, 4)), jnp.float32)
    keys = scatter_about(streams_of[1], (TOKENS, H, DK), 1.0, 6.0, ((0, 32), (1, 4)), jnp.float32)
    values = scatter_about(streams_of[2], (TOKENS, H, DV), 1.0, 6.0, ((0, 32), (1, 4)), jnp.float32)
    entry_gate_logit = draw_entry_gate_logit(jax.random.fold_in(streams_of[6], 71), 0)
    forget_gate = draw_forget_gate(jax.random.fold_in(streams_of[6], 71), 0)
    out_weight = scatter_about(streams_of[5], (H * DV, D), (H * DV) ** -0.5, 0.09375, ((0, 4),))
    return {"queries": queries, "keys": keys, "values": values, "entry_gate_logit": entry_gate_logit, "forget_gate": forget_gate, "out_weight": out_weight}


def block_pass(carry, pieces):
    state_c, state_n, state_m = carry
    q_rows, k_rows, v_rows, gate_in, gate_log = pieces
    size = gate_log.shape[0]
    scale_factor = q_rows.shape[1] ** -0.5
    cum = jnp.cumsum(gate_log)
    logits = cum[:, None] - cum[None, :] + gate_in[None, :]
    lower = jnp.tril(jnp.ones((size, size), dtype=bool))
    logits = jnp.where(lower, logits, -jnp.inf)
    carried = cum + state_m
    top = jnp.maximum(jnp.max(logits, axis=1), carried)
    decays = jnp.exp(logits - top[:, None])
    scores = jnp.dot(q_rows, k_rows.T, precision=lax.Precision.HIGHEST) * scale_factor
    weights = decays * scores
    carry_w = jnp.exp(carried - top)
    num = jnp.dot(weights, v_rows, precision=lax.Precision.HIGHEST)
    num = num + carry_w[:, None] * jnp.dot(q_rows, state_c, precision=lax.Precision.HIGHEST) * scale_factor
    den = jnp.sum(weights, axis=1) + carry_w * jnp.dot(q_rows, state_n, precision=lax.Precision.HIGHEST) * scale_factor
    last = cum[-1]
    keep = last - cum + gate_in
    new_m = jnp.maximum(last + state_m, jnp.max(keep))
    retained_entries = jnp.exp(keep - new_m)[:, None] * k_rows
    old_w = jnp.exp(last + state_m - new_m)
    new_c = old_w * state_c + jnp.dot(retained_entries.T, v_rows, precision=lax.Precision.HIGHEST)
    new_n = old_w * state_n + jnp.sum(retained_entries, axis=0)
    return (new_c, new_n, new_m), (num, den, top)


def reference(queries, keys, values, entry_gate_logit, forget_gate, out_weight):
    block = min(512, TOK_DEV)
    gate_log = jax.nn.log_sigmoid(forget_gate)

    def one_head(pieces):
        q_all, k_all, v_all, gate_in, log_all = pieces
        count = q_all.shape[0] // block
        blocks = (q_all.reshape(count, block, -1), k_all.reshape(count, block, -1),
                  v_all.reshape(count, block, -1), gate_in.reshape(count, block),
                  log_all.reshape(count, block))
        start = (jnp.zeros((q_all.shape[1], v_all.shape[1]), jnp.float32),
                 jnp.zeros((q_all.shape[1],), jnp.float32), jnp.full((), -1e30, jnp.float32))
        final, outputs = lax.scan(block_pass, start, blocks)
        num = outputs[0].reshape(q_all.shape[0], -1)
        den = outputs[1].reshape(q_all.shape[0])
        return (num / jnp.maximum(jnp.abs(den), 1.0)[:, None]).astype(jnp.bfloat16)

    hidden = lax.map(one_head, (jnp.transpose(queries, (1, 0, 2)), jnp.transpose(keys, (1, 0, 2)),
                                jnp.transpose(values, (1, 0, 2)), entry_gate_logit, gate_log))
    hidden = jnp.transpose(hidden, (1, 0, 2)).reshape(TOKENS, H * DV)
    group = H * DV // N_HEAD
    total = jnp.zeros((TOKENS, D), jnp.float32)
    for index in range(N_HEAD):
        part = jnp.dot(hidden[:, index * group:(index + 1) * group], out_weight[index * group:(index + 1) * group],
                       preferred_element_type=jnp.float32).astype(jnp.bfloat16)
        total = total + part.astype(jnp.float32)
    return total.astype(jnp.bfloat16)
```

```python
import functools

import jax
import jax.numpy as jnp
from jax import lax
from jax.experimental import pallas as pl
from jax.experimental.pallas import tpu as pltpu
from jax.sharding import PartitionSpec as P

MESH = pl.DeviceIdType.MESH
F32, BF16 = jnp.float32, jnp.bfloat16
LOW = -1e30


def running(x, join, fill):
    lane = lax.broadcasted_iota(jnp.int32, x.shape, 1)
    step = 1
    while step < x.shape[1]:
        x = join(x, jnp.where(lane >= step, pltpu.roll(x, step, 1), fill))
        step *= 2
    return x


def log_sigmoid(x):
    e = jnp.exp(-jnp.abs(x))
    u = 1.0 + e
    tail = jnp.where(u == 1.0, e, jnp.log(u) * (e / jnp.where(u == 1.0, 1.0, u - 1.0)))
    return jnp.minimum(x, 0.0) - tail


def wide(row, width):
    return jnp.concatenate([row] * (width // row.shape[1]), axis=1)


def mix_kernel(
    q_hbm, k_hbm, v_hbm, gate_in, gate_f, hidden,
    qf, kf, vf, qc, kc, vb, num, den, gcol, grow, own_c, own_n, gone, gone_n, came, came_n,
    chip_c, chip_n, slots, slots_n, back, prefix, pre_n, fix, fix_n, out_c, out_n,
    load_sem, pair_sem, ss, rs, sns, rns, sb, rb,
):
    rows = q_hbm.shape[0]
    tile = 256
    ctx, y = lax.axis_index("ctx"), lax.axis_index("head")
    core = lax.rem(ctx, 2)
    chip = lax.div(ctx, 2)
    mate = ctx + 1 - 2 * core
    chips = slots.shape[0]
    part = slots.shape[1]

    loads = []
    for h in range(2):
        for j, (src, dst) in enumerate(((k_hbm, kf), (v_hbm, vf), (q_hbm, qf))):
            loads.append(pltpu.make_async_copy(src.at[:, h, :], dst.at[h], load_sem.at[h, j]))
    for c in (0, 1, 3, 4, 2, 5):
        loads[c].start()

    barrier = pltpu.get_barrier_semaphore()
    pl.semaphore_signal(barrier, inc=1, device_id=(mate, y), device_id_type=MESH)

    def greet(i, _):
        other = lax.rem(chip + i, chips) * 2 + core
        pl.semaphore_signal(barrier, inc=1, device_id=(other, y), device_id_type=MESH)
        return 0

    lax.fori_loop(1, chips, greet, 0)

    log_f = log_sigmoid(gate_f[...])
    cum = running(log_f, jnp.add, 0.0)
    g = gate_in[...] - cum
    peak = running(g, jnp.maximum, LOW)
    grow[0:2, :] = g
    gcol[...] = jnp.transpose(jnp.concatenate([g, peak, g, peak], axis=0), (1, 0))
    f_end = cum[:, rows - 1:rows]
    g_top = peak[:, rows - 1:rows]

    for h in range(2):
        loads[3 * h].wait()
        loads[3 * h + 1].wait()
        vb[h] = vf[h].astype(BF16)
        w = jnp.exp(gcol[:, h:h + 1] - g_top[h:h + 1, :])
        kw = kf[h] * w
        own_c[h] = lax.dot_general(
            kw.astype(BF16), vb[h], (((0,), (0,)), ((), ())), preferred_element_type=F32
        )
        n = jnp.sum(kw, axis=0, keepdims=True)
        own_n[h, 0:1, :] = n[:, :128]
        own_n[h, 1:2, :] = n[:, 128:]
        own_n[h, 2:3, :] = jnp.broadcast_to(f_end[h:h + 1, :], (1, 128))
        own_n[h, 3:4, :] = jnp.broadcast_to(g_top[h:h + 1, :] + f_end[h:h + 1, :], (1, 128))
        own_n[h, 4:8, :] = jnp.zeros((4, 128), F32)
    pl.semaphore_wait(barrier, chips)
    gone[...] = own_c[1 - core].astype(BF16)
    swap = [
        pltpu.make_async_remote_copy(
            src_ref=gone, dst_ref=came, send_sem=pair_sem.at[0], recv_sem=pair_sem.at[1],
            device_id=(mate, y), device_id_type=MESH),
        pltpu.make_async_remote_copy(
            src_ref=own_n.at[1 - core], dst_ref=came_n, send_sem=pair_sem.at[2], recv_sem=pair_sem.at[3],
            device_id=(mate, y), device_id_type=MESH),
    ]
    for c in swap:
        c.start()
    for c in swap:
        c.wait()

    mine_n, their_n = own_n[core], came_n[...]
    first = core == 0
    n0, n1 = jnp.where(first, mine_n, their_n), jnp.where(first, their_n, mine_n)
    f0, t0, f1, t1 = n0[2:3], n0[3:4], n1[2:3], n1[3:4]
    top = jnp.maximum(t0 + f1, t1)
    w0, w1 = jnp.exp(t0 + f1 - top), jnp.exp(t1 - top)
    w_mine, w_their = jnp.where(first, w0, w1), jnp.where(first, w1, w0)
    width = own_c.shape[2]
    chip_c[...] = (
        own_c[core] * wide(w_mine, width) + came[...].astype(F32) * wide(w_their, width)
    ).astype(BF16)
    chip_n[0:2, :] = n0[0:2] * w0 + n1[0:2] * w1
    chip_n[2:3, :] = f0 + f1
    chip_n[3:4, :] = top
    chip_n[4:8, :] = jnp.zeros((4, 128), F32)

    def to_owner(other):
        at = pl.ds(pl.multiple_of(other * part, part), part)
        who = (other * 2 + core, y)
        return (
            pltpu.make_async_remote_copy(
                src_ref=chip_n, dst_ref=slots_n.at[chip], send_sem=sns.at[other], recv_sem=rns.at[chip],
                device_id=who, device_id_type=MESH),
            pltpu.make_async_remote_copy(
                src_ref=chip_c.at[at], dst_ref=slots.at[chip], send_sem=ss.at[other], recv_sem=rs.at[chip],
                device_id=who, device_id_type=MESH),
        )

    def from_chip(other):
        who = (other * 2 + core, y)
        return (
            pltpu.make_async_remote_copy(
                src_ref=chip_n, dst_ref=slots_n.at[other], send_sem=sns.at[other], recv_sem=rns.at[other],
                device_id=who, device_id_type=MESH),
            pltpu.make_async_remote_copy(
                src_ref=chip_c.at[pl.ds(0, part)], dst_ref=slots.at[other], send_sem=ss.at[other],
                recv_sem=rs.at[other], device_id=who, device_id_type=MESH),
        )

    def send(i, _):
        for c in to_owner(lax.rem(chip + i, chips)):
            c.start()
        return 0

    lax.fori_loop(1, chips, send, 0)
    slots_n[chip] = chip_n[...]
    slots[chip] = chip_c[pl.ds(pl.multiple_of(chip * part, part), part), :]

    def attend(h):
        loads[3 * h + 2].wait()
        q = qf[h] * 0.0625
        q_hi = q.astype(BF16)
        q_lo = (q - q_hi.astype(F32)).astype(BF16)
        qf[h] = q
        qc[h, :, 0:256] = q_hi
        qc[h, :, 256:512] = q_hi
        qc[h, :, 512:768] = q_lo
        k = kf[h]
        k_hi = k.astype(BF16)
        k_lo = (k - k_hi.astype(F32)).astype(BF16)
        kc[:, 0:256] = k_hi
        kc[:, 256:512] = k_lo
        kc[:, 512:768] = k_hi
        for i in range(rows // tile):
            at = slice(i * tile, (i + 1) * tile)
            peak_col = gcol[at, 2 + h:3 + h]
            upto = (i + 1) * tile
            s = lax.dot_general(
                qc[h, at, :], kc[0:upto, :], (((1,), (1,)), ((), ())), preferred_element_type=F32
            )
            z = grow[h:h + 1, 0:upto] - peak_col
            r = lax.broadcasted_iota(jnp.int32, (tile, upto), 0) + i * tile
            c = lax.broadcasted_iota(jnp.int32, (tile, upto), 1)
            w = jnp.exp(jnp.where(c <= r, z, -jnp.inf)) * s
            den[h, at, :] = jnp.sum(w, axis=1, keepdims=True)
            num[h, at, :] = jnp.dot(w.astype(BF16), vb[h, 0:upto, :], preferred_element_type=F32)

    attend(0)

    def got_n(i, _):
        from_chip(lax.rem(chip + i, chips))[0].wait_recv()
        return 0

    lax.fori_loop(1, chips, got_n, 0)

    def got_c(i, _):
        from_chip(lax.rem(chip + i, chips))[1].wait_recv()
        return 0

    lax.fori_loop(1, chips, got_c, 0)

    def give_back(other):
        return pltpu.make_async_remote_copy(
            src_ref=back.at[other], dst_ref=prefix.at[pl.ds(pl.multiple_of(chip * part, part), part)],
            send_sem=sb.at[other], recv_sem=rb.at[chip], device_id=(other * 2 + core, y), device_id_type=MESH)

    def take_back(other):
        return pltpu.make_async_remote_copy(
            src_ref=back.at[other], dst_ref=prefix.at[pl.ds(pl.multiple_of(other * part, part), part)],
            send_sem=sb.at[other], recv_sem=rb.at[other], device_id=(other * 2 + core, y), device_id_type=MESH)

    def scan(p, carry):
        m, c, n = carry
        back[p] = c.astype(BF16)

        @pl.when(p == chip)
        def _():
            pre_n[0:2, :] = n
            pre_n[2:3, :] = m
            prefix[pl.ds(pl.multiple_of(chip * part, part), part), :] = c.astype(BF16)

        @pl.when(p != chip)
        def _():
            give_back(p).start()

        later = slots_n[p]
        f, t = later[2:3], later[3:4]
        top = jnp.maximum(m + f, t)
        a, b = jnp.exp(m + f - top), jnp.exp(t - top)
        c = c * wide(a, width) + slots[p].astype(F32) * wide(b, width)
        return top, c, n * a + later[0:2] * b

    lax.fori_loop(
        0, chips, scan,
        (jnp.full((1, 128), LOW, F32), jnp.zeros((part, width), F32), jnp.zeros((2, 128), F32)),
    )

    attend(1)

    def got_back(i, _):
        take_back(lax.rem(chip + i, chips)).wait_recv()
        return 0

    lax.fori_loop(1, chips, got_back, 0)

    pm, pn = pre_n[2:3, :], pre_n[0:2, :]
    top = jnp.maximum(pm + f0, t0)
    a, b = jnp.exp(pm + f0 - top), jnp.exp(t0 - top)
    zero = jnp.zeros_like(b)
    b_mine, b_their = jnp.where(first, b, zero), jnp.where(first, zero, b)
    p_c = prefix[...].astype(F32)
    second_c = (
        p_c * wide(a, width) + own_c[core] * wide(b_mine, width) + came[...].astype(F32) * wide(b_their, width)
    )
    second_n = pn * a + n0[0:2] * b
    fix[core] = jnp.where(first, p_c, second_c).astype(BF16)
    out_c[...] = jnp.where(first, second_c, p_c).astype(BF16)
    fix_n[core, 0:2, :] = jnp.where(first, pn, second_n)
    fix_n[core, 2:3, :] = jnp.where(first, pm, top)
    out_n[0:2, :] = jnp.where(first, second_n, pn)
    out_n[2:3, :] = jnp.where(first, top, pm)
    out_n[3:8, :] = jnp.zeros((5, 128), F32)
    fix_n[core, 3:8, :] = jnp.zeros((5, 128), F32)
    tell = [
        pltpu.make_async_remote_copy(
            src_ref=out_c, dst_ref=fix.at[core], send_sem=pair_sem.at[4], recv_sem=pair_sem.at[5],
            device_id=(mate, y), device_id_type=MESH),
        pltpu.make_async_remote_copy(
            src_ref=out_n, dst_ref=fix_n.at[core], send_sem=pair_sem.at[6], recv_sem=pair_sem.at[7],
            device_id=(mate, y), device_id_type=MESH),
    ]
    for c in tell:
        c.start()
    for c in tell:
        c.wait()

    for h in range(2):
        pm = fix_n[h, 2:3, 0:1]
        n_row = jnp.concatenate([fix_n[h, 0:1, :], fix_n[h, 1:2, :]], axis=1)
        for i in range(rows // tile):
            at = slice(i * tile, (i + 1) * tile)
            peak_col = gcol[at, 2 + h:3 + h]
            top = jnp.maximum(peak_col, pm)
            ow, iw = jnp.exp(peak_col - top), jnp.exp(pm - top)
            mem = jnp.dot(qc[h, at, 0:256], fix[h], preferred_element_type=F32)
            mem_n = jnp.sum(qf[h, at, :] * n_row, axis=1, keepdims=True)
            d = jnp.maximum(jnp.abs(ow * den[h, at, :] + iw * mem_n), 1.0)
            inv = 1.0 / d
            hidden[at, h * width:(h + 1) * width] = (
                (ow * inv) * num[h, at, :] + (iw * inv) * mem
            ).astype(BF16)

    def sent(i, _):
        other = lax.rem(chip + i, chips)
        for c in to_owner(other):
            c.wait_send()
        give_back(other).wait_send()
        return 0

    lax.fori_loop(1, chips, sent, 0)


def mix(queries, keys, values, gate_in, gate_f):
    rows, heads, dk = queries.shape
    dv = values.shape[2]
    chips = lax.axis_size("ctx") // 2
    part = dk // chips
    hbm = pl.BlockSpec(memory_space=pl.ANY)
    vmem = pl.BlockSpec(memory_space=pltpu.VMEM)
    V = pltpu.VMEM
    dma = pltpu.SemaphoreType.DMA
    return pl.pallas_call(
        mix_kernel,
        out_shape=jax.ShapeDtypeStruct((rows, heads * dv), BF16),
        in_specs=[hbm, hbm, hbm, vmem, vmem],
        out_specs=vmem,
        scratch_shapes=[
            V((heads, rows, dk), F32), V((heads, rows, dk), F32), V((heads, rows, dv), F32),
            V((heads, rows, 3 * dk), BF16), V((rows, 3 * dk), BF16), V((heads, rows, dv), BF16),
            V((heads, rows, dv), F32), V((heads, rows, 1), F32), V((rows, 8), F32), V((8, rows), F32),
            V((heads, dk, dv), F32), V((heads, 8, 128), F32), V((dk, dv), BF16), V((8, 128), F32),
            V((dk, dv), BF16), V((8, 128), F32),
            V((dk, dv), BF16), V((8, 128), F32), V((chips, part, dv), BF16), V((chips, 8, 128), F32),
            V((chips, part, dv), BF16), V((dk, dv), BF16), V((8, 128), F32),
            V((heads, dk, dv), BF16), V((heads, 8, 128), F32), V((dk, dv), BF16), V((8, 128), F32),
            dma((heads, 3)), dma((8,)), dma((chips,)), dma((chips,)), dma((chips,)), dma((chips,)),
            dma((chips,)), dma((chips,)),
        ],
        compiler_params=pltpu.CompilerParams(
            collective_id=0, has_side_effects=True, vmem_limit_bytes=60 << 20
        ),
        name="mix",
    )(queries, keys, values, gate_in, gate_f)


def on_device(queries, keys, values, entry_gate_logit, forget_gate, out_weight):
    hidden = mix(queries, keys, values, entry_gate_logit, forget_gate)
    terms = jnp.dot(hidden, out_weight, preferred_element_type=F32)
    return lax.psum_scatter(terms.astype(BF16), "head", scatter_dimension=1, tiled=True)


def solution(mesh):
    placed = (
        P("ctx", "head", None),
        P("ctx", "head", None),
        P("ctx", "head", None),
        P("head", "ctx"),
        P("head", "ctx"),
        P("head", None),
    )
    return jax.shard_map(
        on_device, mesh=mesh, in_specs=placed, out_specs=P("ctx", "head"), check_vma=False
    )
```

```python
import functools

import jax
import jax.numpy as jnp
from jax import lax
from jax.experimental import pallas as pl
from jax.experimental.pallas import tpu as pltpu
from jax.sharding import PartitionSpec as P

MESH = pl.DeviceIdType.MESH
F32, BF16 = jnp.float32, jnp.bfloat16
LOW = -1e30


def running(x, join, fill):
    lane = lax.broadcasted_iota(jnp.int32, x.shape, 1)
    step = 1
    while step < x.shape[1]:
        x = join(x, jnp.where(lane >= step, pltpu.roll(x, step, 1), fill))
        step *= 2
    return x


def log_sigmoid(x):
    e = jnp.exp(-jnp.abs(x))
    u = 1.0 + e
    tail = jnp.where(u == 1.0, e, jnp.log(u) * (e / jnp.where(u == 1.0, 1.0, u - 1.0)))
    return jnp.minimum(x, 0.0) - tail


def wide(row, width):
    return jnp.concatenate([row] * (width // row.shape[1]), axis=1)


def layer_kernel(
    q_hbm, k_hbm, v_hbm, w_hbm, gate_in, gate_f, out,
    qf, kf, vf, qc, kc, vb, num, den, gcol, grow, own_c, own_n, gone, gone_n, came, came_n,
    chip_c, chip_n, slots, slots_n, back, prefix, pre_n, fix, fix_n, out_c, out_n,
    hidden, swapped, w_own, w_mate, y_out, y_in, z_out,
    load_sem, pair_sem, ss, rs, sns, rns, sb, rb,
    fetch_s, fetch_r, ring_s, ring_r, share_s, share_r, xs, xr, ys, yr, zs, zr,
):
    rows = q_hbm.shape[0]
    tile = 256
    ctx, y = lax.axis_index("ctx"), lax.axis_index("head")
    core = lax.rem(ctx, 2)
    chip = lax.div(ctx, 2)
    mate = ctx + 1 - 2 * core
    chips = slots.shape[0]
    part = slots.shape[1]
    side = lax.rem(y, 2)
    pair = lax.div(y, 2)
    partner = y + 1 - 2 * side
    across = 3 - y
    kept = lax.rem(lax.div(y + 1, 2), 2)
    cx, cz = lax.rem(chip, 4), lax.div(chip, 4)
    half = rows // 2
    cols = w_own.shape[2]
    block = cols // 2

    loads = []
    for h in range(2):
        for j, (src, dst) in enumerate(((k_hbm, kf), (v_hbm, vf), (q_hbm, qf))):
            loads.append(pltpu.make_async_copy(src.at[:, h, :], dst.at[h], load_sem.at[h, j]))
    for c in (0, 1, 3, 4, 2, 5):
        loads[c].start()
    w_loads = [
        pltpu.make_async_copy(
            w_hbm.at[:, pl.ds(pl.multiple_of((1 - pair if f == 0 else pair) * cols, cols), cols)],
            w_own.at[f], load_sem.at[2, f])
        for f in range(2)
    ]
    for c in w_loads:
        c.start()

    barrier = pltpu.get_barrier_semaphore()
    for who in ((mate, y), (ctx, partner), (ctx, across)):
        pl.semaphore_signal(barrier, inc=1, device_id=who, device_id_type=MESH)

    def greet(i, _):
        other = lax.rem(chip + i, chips) * 2 + core
        pl.semaphore_signal(barrier, inc=1, device_id=(other, y), device_id_type=MESH)
        return 0

    lax.fori_loop(1, chips, greet, 0)

    def strip(path, z_at, x_at, count=1):
        at = z_at * 4 + x_at if path == 0 else x_at * 4 + z_at
        return pl.ds(pl.multiple_of((core * 2 + path) * 256 + at * 16, 16), 16 * count)

    def fetch(f, path):
        at = strip(path, cz, cx)
        col = (1 - pair if f == 0 else pair) * cols
        return pltpu.make_async_remote_copy(
            src_ref=w_hbm.at[at, pl.ds(pl.multiple_of(col, cols), cols)], dst_ref=w_mate.at[f, at],
            send_sem=fetch_s.at[f, path], recv_sem=fetch_r.at[f, path], device_id=(ctx, partner), device_id_type=MESH)

    def ring(f, path, stage, step, way, incoming):
        along_x = (path == 0) == (stage == 0)
        here = cx if along_x else cz
        to = lax.rem(here + (1 if way == 0 else 3), 4)
        back_by = step + (1 if incoming else 0)
        owner = lax.rem(here + (4 - back_by if way == 0 else back_by), 4)
        if stage == 0:
            at = strip(path, cz, owner) if along_x else strip(path, owner, cx)
        else:
            at = strip(path, 0, owner, 4) if along_x else strip(path, owner, 0, 4)
        width = cols if step == 0 else block
        lo = 0 if step == 0 else way * block
        ref = w_mate.at[f, at, pl.ds(lo, width)]
        peer = (cz * 4 + to if along_x else to * 4 + cx) * 2 + core
        i = stage * 4 + step * 2 + way
        return pltpu.make_async_remote_copy(
            src_ref=ref, dst_ref=ref, send_sem=ring_s.at[f, path, i], recv_sem=ring_r.at[f, path, i],
            device_id=(peer, y), device_id_type=MESH)

    def share(f, who):
        ref = w_mate.at[f, pl.ds(pl.multiple_of(who * 512, 512), 512)]
        return pltpu.make_async_remote_copy(
            src_ref=ref, dst_ref=ref, send_sem=share_s.at[f], recv_sem=share_r.at[f],
            device_id=(mate, y), device_id_type=MESH)

    def gather(f, at):
        if at == 0:
            for path in range(2):
                fetch(f, path).start()
        for path in range(2):
            if at == 1:
                fetch(f, path).wait_recv()
            if 2 <= at <= 5:
                for way in range(2):
                    ring(f, path, (at - 2) // 2, (at - 2) % 2, way, True).wait_recv()
            if 1 <= at <= 4:
                for way in range(2):
                    ring(f, path, (at - 1) // 2, (at - 1) % 2, way, False).start()
        if at == 5:
            share(f, core).start()
        if at == 6:
            share(f, 1 - core).wait_recv()

    def gather_sent(f):
        for path in range(2):
            fetch(f, path).wait_send()
            for i in range(8):
                ring(f, path, i // 4, (i // 2) % 2, i % 2, False).wait_send()
        share(f, core).wait_send()

    log_f = log_sigmoid(gate_f[...])
    cum = running(log_f, jnp.add, 0.0)
    g = gate_in[...] - cum
    peak = running(g, jnp.maximum, LOW)
    grow[0:2, :] = g
    gcol[...] = jnp.transpose(jnp.concatenate([g, peak, g, peak], axis=0), (1, 0))
    f_end = cum[:, rows - 1:rows]
    pl.semaphore_wait(barrier, chips + 2)
    gather(0, 0)
    gather(1, 0)
    g_top = peak[:, rows - 1:rows]

    for h in range(2):
        loads[3 * h].wait()
        loads[3 * h + 1].wait()
        vb[h] = vf[h].astype(BF16)
        w = jnp.exp(gcol[:, h:h + 1] - g_top[h:h + 1, :])
        kw = kf[h] * w
        own_c[h] = lax.dot_general(
            kw.astype(BF16), vb[h], (((0,), (0,)), ((), ())), preferred_element_type=F32
        )
        n = jnp.sum(kw, axis=0, keepdims=True)
        own_n[h, 0:1, :] = n[:, :128]
        own_n[h, 1:2, :] = n[:, 128:]
        own_n[h, 2:3, :] = jnp.broadcast_to(f_end[h:h + 1, :], (1, 128))
        own_n[h, 3:4, :] = jnp.broadcast_to(g_top[h:h + 1, :] + f_end[h:h + 1, :], (1, 128))
        own_n[h, 4:8, :] = jnp.zeros((4, 128), F32)
    gather(0, 1)
    gone[...] = own_c[1 - core].astype(BF16)
    swap = [
        pltpu.make_async_remote_copy(
            src_ref=gone, dst_ref=came, send_sem=pair_sem.at[0], recv_sem=pair_sem.at[1],
            device_id=(mate, y), device_id_type=MESH),
        pltpu.make_async_remote_copy(
            src_ref=own_n.at[1 - core], dst_ref=came_n, send_sem=pair_sem.at[2], recv_sem=pair_sem.at[3],
            device_id=(mate, y), device_id_type=MESH),
    ]
    for c in swap:
        c.start()
    for c in swap:
        c.wait()

    mine_n, their_n = own_n[core], came_n[...]
    first = core == 0
    n0, n1 = jnp.where(first, mine_n, their_n), jnp.where(first, their_n, mine_n)
    f0, t0, f1, t1 = n0[2:3], n0[3:4], n1[2:3], n1[3:4]
    top = jnp.maximum(t0 + f1, t1)
    w0, w1 = jnp.exp(t0 + f1 - top), jnp.exp(t1 - top)
    w_mine, w_their = jnp.where(first, w0, w1), jnp.where(first, w1, w0)
    width = own_c.shape[2]
    chip_c[...] = (
        own_c[core] * wide(w_mine, width) + came[...].astype(F32) * wide(w_their, width)
    ).astype(BF16)
    chip_n[0:2, :] = n0[0:2] * w0 + n1[0:2] * w1
    chip_n[2:3, :] = f0 + f1
    chip_n[3:4, :] = top
    chip_n[4:8, :] = jnp.zeros((4, 128), F32)

    def to_owner(other):
        at = pl.ds(pl.multiple_of(other * part, part), part)
        who = (other * 2 + core, y)
        return (
            pltpu.make_async_remote_copy(
                src_ref=chip_n, dst_ref=slots_n.at[chip], send_sem=sns.at[other], recv_sem=rns.at[chip],
                device_id=who, device_id_type=MESH),
            pltpu.make_async_remote_copy(
                src_ref=chip_c.at[at], dst_ref=slots.at[chip], send_sem=ss.at[other], recv_sem=rs.at[chip],
                device_id=who, device_id_type=MESH),
        )

    def from_chip(other):
        who = (other * 2 + core, y)
        return (
            pltpu.make_async_remote_copy(
                src_ref=chip_n, dst_ref=slots_n.at[other], send_sem=sns.at[other], recv_sem=rns.at[other],
                device_id=who, device_id_type=MESH),
            pltpu.make_async_remote_copy(
                src_ref=chip_c.at[pl.ds(0, part)], dst_ref=slots.at[other], send_sem=ss.at[other],
                recv_sem=rs.at[other], device_id=who, device_id_type=MESH),
        )

    def send(i, _):
        for c in to_owner(lax.rem(chip + i, chips)):
            c.start()
        return 0

    lax.fori_loop(1, chips, send, 0)
    gather(0, 2)
    slots_n[chip] = chip_n[...]
    slots[chip] = chip_c[pl.ds(pl.multiple_of(chip * part, part), part), :]

    def attend(h, between):
        loads[3 * h + 2].wait()
        q = qf[h] * 0.0625
        q_hi = q.astype(BF16)
        q_lo = (q - q_hi.astype(F32)).astype(BF16)
        qf[h] = q
        qc[h, :, 0:256] = q_hi
        qc[h, :, 256:512] = q_hi
        qc[h, :, 512:768] = q_lo
        k = kf[h]
        k_hi = k.astype(BF16)
        k_lo = (k - k_hi.astype(F32)).astype(BF16)
        kc[:, 0:256] = k_hi
        kc[:, 256:512] = k_lo
        kc[:, 512:768] = k_hi
        for i in range(rows // tile):
            at = slice(i * tile, (i + 1) * tile)
            peak_col = gcol[at, 2 + h:3 + h]
            upto = (i + 1) * tile
            s = lax.dot_general(
                qc[h, at, :], kc[0:upto, :], (((1,), (1,)), ((), ())), preferred_element_type=F32
            )
            z = grow[h:h + 1, 0:upto] - peak_col
            r = lax.broadcasted_iota(jnp.int32, (tile, upto), 0) + i * tile
            c = lax.broadcasted_iota(jnp.int32, (tile, upto), 1)
            w = jnp.exp(jnp.where(c <= r, z, -jnp.inf)) * s
            den[h, at, :] = jnp.sum(w, axis=1, keepdims=True)
            num[h, at, :] = jnp.dot(w.astype(BF16), vb[h, 0:upto, :], preferred_element_type=F32)
            if i == 2:
                gather(0, between)

    attend(0, 3)
    gather(0, 4)

    def got_n(i, _):
        from_chip(lax.rem(chip + i, chips))[0].wait_recv()
        return 0

    lax.fori_loop(1, chips, got_n, 0)

    def got_c(i, _):
        from_chip(lax.rem(chip + i, chips))[1].wait_recv()
        return 0

    lax.fori_loop(1, chips, got_c, 0)

    def give_back(other):
        return pltpu.make_async_remote_copy(
            src_ref=back.at[other], dst_ref=prefix.at[pl.ds(pl.multiple_of(chip * part, part), part)],
            send_sem=sb.at[other], recv_sem=rb.at[chip], device_id=(other * 2 + core, y), device_id_type=MESH)

    def take_back(other):
        return pltpu.make_async_remote_copy(
            src_ref=back.at[other], dst_ref=prefix.at[pl.ds(pl.multiple_of(other * part, part), part)],
            send_sem=sb.at[other], recv_sem=rb.at[other], device_id=(other * 2 + core, y), device_id_type=MESH)

    def scan(p, carry):
        m, c, n = carry
        back[p] = c.astype(BF16)

        @pl.when(p == chip)
        def _():
            pre_n[0:2, :] = n
            pre_n[2:3, :] = m
            prefix[pl.ds(pl.multiple_of(chip * part, part), part), :] = c.astype(BF16)

        @pl.when(p != chip)
        def _():
            give_back(p).start()

        later = slots_n[p]
        f, t = later[2:3], later[3:4]
        top = jnp.maximum(m + f, t)
        a, b = jnp.exp(m + f - top), jnp.exp(t - top)
        c = c * wide(a, width) + slots[p].astype(F32) * wide(b, width)
        return top, c, n * a + later[0:2] * b

    lax.fori_loop(
        0, chips, scan,
        (jnp.full((1, 128), LOW, F32), jnp.zeros((part, width), F32), jnp.zeros((2, 128), F32)),
    )

    attend(1, 5)
    gather(1, 1)

    def got_back(i, _):
        take_back(lax.rem(chip + i, chips)).wait_recv()
        return 0

    lax.fori_loop(1, chips, got_back, 0)

    pm, pn = pre_n[2:3, :], pre_n[0:2, :]
    top = jnp.maximum(pm + f0, t0)
    a, b = jnp.exp(pm + f0 - top), jnp.exp(t0 - top)
    zero = jnp.zeros_like(b)
    b_mine, b_their = jnp.where(first, b, zero), jnp.where(first, zero, b)
    p_c = prefix[...].astype(F32)
    second_c = (
        p_c * wide(a, width) + own_c[core] * wide(b_mine, width) + came[...].astype(F32) * wide(b_their, width)
    )
    second_n = pn * a + n0[0:2] * b
    fix[core] = jnp.where(first, p_c, second_c).astype(BF16)
    out_c[...] = jnp.where(first, second_c, p_c).astype(BF16)
    fix_n[core, 0:2, :] = jnp.where(first, pn, second_n)
    fix_n[core, 2:3, :] = jnp.where(first, pm, top)
    out_n[0:2, :] = jnp.where(first, second_n, pn)
    out_n[2:3, :] = jnp.where(first, top, pm)
    out_n[3:8, :] = jnp.zeros((5, 128), F32)
    fix_n[core, 3:8, :] = jnp.zeros((5, 128), F32)
    tell = [
        pltpu.make_async_remote_copy(
            src_ref=out_c, dst_ref=fix.at[core], send_sem=pair_sem.at[4], recv_sem=pair_sem.at[5],
            device_id=(mate, y), device_id_type=MESH),
        pltpu.make_async_remote_copy(
            src_ref=out_n, dst_ref=fix_n.at[core], send_sem=pair_sem.at[6], recv_sem=pair_sem.at[7],
            device_id=(mate, y), device_id_type=MESH),
    ]
    for c in tell:
        c.start()
    for c in tell:
        c.wait()

    gather(1, 2)

    def finish(start, count):
        at = pl.ds(pl.multiple_of(start, 64), count)
        for h in range(2):
            pm = fix_n[h, 2:3, 0:1]
            n_row = jnp.concatenate([fix_n[h, 0:1, :], fix_n[h, 1:2, :]], axis=1)
            peak_col = gcol[at, 2 + h:3 + h]
            top = jnp.maximum(peak_col, pm)
            ow, iw = jnp.exp(peak_col - top), jnp.exp(pm - top)
            mem = jnp.dot(qc[h, at, 0:256], fix[h], preferred_element_type=F32)
            mem_n = jnp.sum(qf[h, at, :] * n_row, axis=1, keepdims=True)
            d = jnp.maximum(jnp.abs(ow * den[h, at, :] + iw * mem_n), 1.0)
            inv = 1.0 / d
            hidden[at, h * width:(h + 1) * width] = (
                (ow * inv) * num[h, at, :] + (iw * inv) * mem
            ).astype(BF16)

    chunks = ((0, 64, 1024), (64, 64, 1024), (128, 128, 512), (256, 256, 256))
    y_first = (0, 2, 4, 8)

    def x_copy(c):
        start, count, _ = chunks[c]
        src = hidden.at[pl.ds(pl.multiple_of((1 - kept) * half + start, 64), count)]
        return pltpu.make_async_remote_copy(
            src_ref=src, dst_ref=swapped.at[pl.ds(start, count)], send_sem=xs.at[c], recv_sem=xr.at[c],
            device_id=(ctx, partner), device_id_type=MESH)

    def y_copy(c, j, first):
        start, count, w = chunks[c]
        col = pl.multiple_of(lax.rem(first * block + j * w, cols), w)
        at = (pl.ds(start, count), pl.ds(col, w))
        return pltpu.make_async_remote_copy(
            src_ref=y_out.at[at], dst_ref=y_in.at[at], send_sem=ys.at[y_first[c] + j],
            recv_sem=yr.at[y_first[c] + j], device_id=(ctx, across), device_id_type=MESH)

    def z_copy(c, j, incoming):
        start, count, w = chunks[c]
        rows_at = (1 - kept if incoming else kept) * half + start
        return pltpu.make_async_remote_copy(
            src_ref=z_out.at[pl.ds(start, count), pl.ds(pl.multiple_of(j * w, w), w)],
            dst_ref=out.at[pl.ds(pl.multiple_of(rows_at, 64), count), pl.ds(pl.multiple_of(j * w, w), w)],
            send_sem=zs.at[y_first[c] // 2 + j], recv_sem=zr.at[y_first[c] // 2 + j],
            device_id=(ctx, partner), device_id_type=MESH)

    def project(c, f, col):
        start, count, w = chunks[c]
        at = pl.ds(pl.multiple_of(kept * half + start, 64), count)
        return jnp.dot(hidden[at, :], w_own[f, :, pl.ds(col, w)], preferred_element_type=F32) + jnp.dot(
            swapped[pl.ds(start, count), :], w_mate[f, :, pl.ds(col, w)], preferred_element_type=F32)

    def y_step(c):
        start, count, w = chunks[c]
        x_copy(c).wait_recv()

        def one(j, _):
            col = pl.multiple_of(lax.rem(side * block + j * w, cols), w)
            y_out[pl.ds(start, count), pl.ds(col, w)] = project(c, 0, col).astype(BF16)
            y_copy(c, j, side).start()
            return 0

        lax.fori_loop(0, cols // w, one, 0)

    def f_step(c):
        start, count, w = chunks[c]
        per = block // w

        def for_partner(j, _):
            col = pl.multiple_of((1 - side) * block + j * w, w)
            mine = project(c, 1, col)
            y_copy(c, j, 1 - side).wait_recv()
            z_out[pl.ds(start, count), pl.ds(pl.multiple_of(j * w, w), w)] = (
                mine + y_in[pl.ds(start, count), pl.ds(col, w)].astype(F32)).astype(BF16)
            z_copy(c, j, False).start()
            return 0

        lax.fori_loop(0, per, for_partner, 0)

        def for_me(j, _):
            col = pl.multiple_of(side * block + j * w, w)
            mine = project(c, 1, col)
            y_copy(c, j + per, 1 - side).wait_recv()
            at = pl.ds(pl.multiple_of(kept * half + start, 64), count)
            out[at, pl.ds(pl.multiple_of(j * w, w), w)] = (
                mine + y_in[pl.ds(start, count), pl.ds(col, w)].astype(F32)).astype(BF16)
            return 0

        lax.fori_loop(0, per, for_me, 0)

    for c in range(4):
        finish((1 - kept) * half + chunks[c][0], chunks[c][1])
        x_copy(c).start()
        if c == 1:
            finish(kept * half + chunks[0][0], chunks[0][1])
    gather(1, 3)
    for c in range(1, 4):
        finish(kept * half + chunks[c][0], chunks[c][1])
    w_loads[0].wait()
    gather(0, 6)
    y_step(0)
    y_step(1)
    gather(1, 4)
    y_step(2)
    gather(1, 5)
    w_loads[1].wait()
    gather(1, 6)
    f_step(0)
    f_step(1)
    y_step(3)
    f_step(2)
    f_step(3)

    gather_sent(0)
    gather_sent(1)
    for c in range(4):
        x_copy(c).wait_send()
        per = block // chunks[c][2]

        def y_sent(j, _, c=c):
            y_copy(c, j, side).wait_send()
            return 0

        def z_done(j, _, c=c):
            z_copy(c, j, False).wait_send()
            z_copy(c, j, True).wait_recv()
            return 0

        lax.fori_loop(0, 2 * per, y_sent, 0)
        lax.fori_loop(0, per, z_done, 0)

    def sent(i, _):
        other = lax.rem(chip + i, chips)
        for c in to_owner(other):
            c.wait_send()
        give_back(other).wait_send()
        return 0

    lax.fori_loop(1, chips, sent, 0)


def layer(queries, keys, values, out_weight, gate_in, gate_f):
    rows, heads, dk = queries.shape
    dv = values.shape[2]
    chips = lax.axis_size("ctx") // 2
    part = dk // chips
    hbm = pl.BlockSpec(memory_space=pl.ANY)
    vmem = pl.BlockSpec(memory_space=pltpu.VMEM)
    V = pltpu.VMEM
    dma = pltpu.SemaphoreType.DMA
    return pl.pallas_call(
        layer_kernel,
        out_shape=jax.ShapeDtypeStruct((rows, out_weight.shape[1] // 4), BF16),
        in_specs=[hbm, hbm, hbm, hbm, vmem, vmem],
        out_specs=vmem,
        scratch_shapes=[
            V((heads, rows, dk), F32), V((heads, rows, dk), F32), V((heads, rows, dv), F32),
            V((heads, rows, 3 * dk), BF16), V((rows, 3 * dk), BF16), V((heads, rows, dv), BF16),
            V((heads, rows, dv), F32), V((heads, rows, 1), F32), V((rows, 8), F32), V((8, rows), F32),
            V((heads, dk, dv), F32), V((heads, 8, 128), F32), V((dk, dv), BF16), V((8, 128), F32),
            V((dk, dv), BF16), V((8, 128), F32),
            V((dk, dv), BF16), V((8, 128), F32), V((chips, part, dv), BF16), V((chips, 8, 128), F32),
            V((chips, part, dv), BF16), V((dk, dv), BF16), V((8, 128), F32),
            V((heads, dk, dv), BF16), V((heads, 8, 128), F32), V((dk, dv), BF16), V((8, 128), F32),
            V((rows, heads * dv), BF16), V((rows // 2, heads * dv), BF16),
            V((2, heads * dv, out_weight.shape[1] // 2), BF16), V((2, heads * dv, out_weight.shape[1] // 2), BF16),
            V((rows // 2, out_weight.shape[1] // 2), BF16), V((rows // 2, out_weight.shape[1] // 2), BF16),
            V((rows // 2, out_weight.shape[1] // 4), BF16),
            dma((3, 3)), dma((8,)), dma((chips,)), dma((chips,)), dma((chips,)), dma((chips,)),
            dma((chips,)), dma((chips,)),
            dma((2, 2)), dma((2, 2)), dma((2, 2, 8)), dma((2, 2, 8)), dma((2,)), dma((2,)),
            dma((4,)), dma((4,)), dma((16,)), dma((16,)), dma((8,)), dma((8,)),
        ],
        compiler_params=pltpu.CompilerParams(
            collective_id=0, has_side_effects=True, vmem_limit_bytes=60 << 20
        ),
        name="layer",
    )(queries, keys, values, out_weight, gate_in, gate_f)


def on_device(queries, keys, values, entry_gate_logit, forget_gate, out_weight):
    return layer(queries, keys, values, out_weight, entry_gate_logit, forget_gate)


def solution(mesh):
    placed = (
        P("ctx", "head", None),
        P("ctx", "head", None),
        P("ctx", "head", None),
        P("head", "ctx"),
        P("head", "ctx"),
        P("head", None),
    )
    return jax.shard_map(
        on_device, mesh=mesh, in_specs=placed, out_specs=P("ctx", "head"), check_vma=False
    )
```

```python
import functools

import jax
import jax.numpy as jnp
from jax import lax
from jax.experimental import pallas as pl
from jax.experimental.pallas import tpu as pltpu
from jax.sharding import PartitionSpec as P

MESH = pl.DeviceIdType.MESH
F32, BF16 = jnp.float32, jnp.bfloat16
LOW = -1e30


def running(x, join, fill):
    lane = lax.broadcasted_iota(jnp.int32, x.shape, 1)
    row = lax.broadcasted_iota(jnp.int32, x.shape, 0)
    for step in (1, 2, 4, 8, 16, 32, 64):
        x = join(x, jnp.where(lane >= step, pltpu.roll(x, step, 1), fill))
    ends = jnp.broadcast_to(x[:, 127:128], x.shape)
    ends = jnp.where(row >= 2, pltpu.roll(ends, 2, 0), fill)
    for step in (2, 4, 8):
        ends = join(ends, jnp.where(row >= step, pltpu.roll(ends, step, 0), fill))
    return join(x, ends)


def stacked(x):
    return jnp.concatenate([x[:, j:j + 128] for j in range(0, x.shape[1], 128)], axis=0)


def unstacked(x):
    return jnp.concatenate([x[j:j + 2, :] for j in range(0, x.shape[0], 2)], axis=1)


def log_sigmoid(x):
    e = jnp.exp(-jnp.abs(x))
    u = 1.0 + e
    tail = jnp.where(u == 1.0, e, jnp.log(u) * (e / jnp.where(u == 1.0, 1.0, u - 1.0)))
    return jnp.minimum(x, 0.0) - tail


def wide(row, width):
    return jnp.concatenate([row] * (width // row.shape[1]), axis=1)


def layer_kernel(
    q_hbm, k_hbm, v_hbm, w_hbm, gate_in, gate_f, out,
    qf, kf, vf, qc, kc, vb, num, den, gcol, grow, own_c, own_n, gone, gone_n, came, came_n,
    chip_c, chip_n, slots, slots_n, back, prefix, pre_n, fix, fix_n, out_c, out_n,
    hidden, swapped, w_own, w_mate, y_out, y_in, z_out,
    load_sem, w_sem, pair_sem, ss, rs, sns, rns, sb, rb,
    fetch_s, fetch_r, ring_s, ring_r, share_s, share_r, xs, xr, ys, yr, zs, zr,
):
    rows = q_hbm.shape[0]
    tile = 256
    ctx, y = lax.axis_index("ctx"), lax.axis_index("head")
    core = lax.rem(ctx, 2)
    chip = lax.div(ctx, 2)
    mate = ctx + 1 - 2 * core
    chips = slots.shape[0]
    part = slots.shape[1]
    side = lax.rem(y, 2)
    pair = lax.div(y, 2)
    partner = y + 1 - 2 * side
    across = 3 - y
    kept = lax.rem(lax.div(y + 1, 2), 2)
    cx, cz = lax.rem(chip, 4), lax.div(chip, 4)
    half = rows // 2
    block = w_own.shape[2]

    def column(b, part_of, of_y):
        other = of_y + 1 - 2 * part_of
        start = (lax.div(of_y, 2) * -2 + 2 + part_of, lax.div(of_y, 2) * -2 + 3 - part_of, other, of_y)[b]
        return start * block

    barrier = pltpu.get_barrier_semaphore()
    for who in ((mate, y), (ctx, partner), (ctx, across)):
        pl.semaphore_signal(barrier, inc=1, device_id=who, device_id_type=MESH)

    def greet(i, _):
        other = lax.rem(chip + i, chips) * 2 + core
        pl.semaphore_signal(barrier, inc=1, device_id=(other, y), device_id_type=MESH)
        return 0

    lax.fori_loop(1, chips, greet, 0)

    loads = []
    for h in range(2):
        for j, (src, dst) in enumerate(((k_hbm, kf), (v_hbm, vf), (q_hbm, qf))):
            loads.append(pltpu.make_async_copy(src.at[:, h, :], dst.at[h], load_sem.at[h, j]))
    for c in (0, 1, 3, 4, 2, 5):
        loads[c].start()
    w_loads = [
        pltpu.make_async_copy(
            w_hbm.at[:, pl.ds(pl.multiple_of(column(b, side, y), block), block)], w_own.at[b], w_sem.at[b])
        for b in range(4)
    ]

    parts = ((0, 0, block // 2), (0, block // 2, block // 2), (1, 0, block), (2, 0, block), (3, 0, block))

    def strip(f, path, z_at, x_at, count):
        at = z_at * 4 + x_at if path == 0 else x_at * 4 + z_at
        b, lo, width = parts[f]
        return w_mate.at[
            b, pl.ds(pl.multiple_of((core * 2 + path) * 256 + at * 16, 16), 16 * count), pl.ds(lo, width)]

    def fetch(f, path):
        at = cz * 4 + cx if path == 0 else cx * 4 + cz
        b, lo, width = parts[f]
        col = column(b, 1 - side, partner) + lo
        return pltpu.make_async_remote_copy(
            src_ref=w_hbm.at[
                pl.ds(pl.multiple_of((core * 2 + path) * 256 + at * 16, 16), 16),
                pl.ds(pl.multiple_of(col, 128), width)],
            dst_ref=strip(f, path, cz, cx, 1),
            send_sem=fetch_s.at[f, path], recv_sem=fetch_r.at[f, path], device_id=(ctx, partner), device_id_type=MESH)

    def spread(f, path, stage, way, incoming):
        along_x = (path == 0) == (stage == 0)
        here = cx if along_x else cz
        to = lax.rem(here + way, 4)
        owner = lax.rem(here + 4 - way, 4) if incoming else here
        if stage == 0:
            ref = strip(f, path, cz, owner, 1) if along_x else strip(f, path, owner, cx, 1)
        else:
            ref = strip(f, path, 0, owner, 4) if along_x else strip(f, path, owner, 0, 4)
        peer = (cz * 4 + to if along_x else to * 4 + cx) * 2 + core
        i = stage * 3 + way - 1
        return pltpu.make_async_remote_copy(
            src_ref=ref, dst_ref=ref, send_sem=ring_s.at[f, path, i], recv_sem=ring_r.at[f, path, i],
            device_id=(peer, y), device_id_type=MESH)

    def share(f, who):
        b, lo, width = parts[f]
        ref = w_mate.at[b, pl.ds(pl.multiple_of(who * 512, 512), 512), pl.ds(lo, width)]
        return pltpu.make_async_remote_copy(
            src_ref=ref, dst_ref=ref, send_sem=share_s.at[f], recv_sem=share_r.at[f],
            device_id=(mate, y), device_id_type=MESH)

    def gather(f, *steps):
        for step in steps:
            for path in range(2):
                if step == 0:
                    fetch(f, path).start()
                if step == 1:
                    fetch(f, path).wait_recv()
                for way in (1, 3, 2):
                    if step == 2 or step == 3:
                        spread(f, path, step - 2, way, True).wait_recv()
                for way in (1, 3, 2):
                    if step == 1 or step == 2:
                        spread(f, path, step - 1, way, False).start()
            if step == 3:
                share(f, core).start()
            if step == 4:
                share(f, 1 - core).wait_recv()

    def gather_sent(f):
        for path in range(2):
            fetch(f, path).wait_send()
            for i in range(6):
                spread(f, path, i // 3, i % 3 + 1, False).wait_send()
        share(f, core).wait_send()

    pl.semaphore_wait(barrier, chips + 2)
    gather(0, 0)
    gather(1, 0)
    for c in w_loads:
        c.start()
    cum = running(log_sigmoid(stacked(gate_f[...])), jnp.add, 0.0)
    g = stacked(gate_in[...]) - cum
    peak = running(g, jnp.maximum, LOW)
    f_end = cum[14:16, 127:128]
    g_top = peak[14:16, 127:128]
    g, peak = unstacked(g), unstacked(peak)
    grow[0:2, :] = g
    gcol[...] = jnp.transpose(jnp.concatenate([g, peak, g, peak], axis=0), (1, 0))
    for c in (0, 1, 3, 4):
        loads[c].wait()
    swap = [
        pltpu.make_async_remote_copy(
            src_ref=gone, dst_ref=came, send_sem=pair_sem.at[0], recv_sem=pair_sem.at[1],
            device_id=(mate, y), device_id_type=MESH),
        pltpu.make_async_remote_copy(
            src_ref=own_n.at[1 - core], dst_ref=came_n, send_sem=pair_sem.at[2], recv_sem=pair_sem.at[3],
            device_id=(mate, y), device_id_type=MESH),
    ]
    for turn, h in enumerate((1 - core, core)):
        lead = h == 0
        vb[h] = vf[h].astype(BF16)
        top = jnp.where(lead, g_top[0:1, :], g_top[1:2, :])
        end = jnp.where(lead, f_end[0:1, :], f_end[1:2, :])
        w = jnp.exp(jnp.where(lead, gcol[:, 0:1], gcol[:, 1:2]) - top)
        kw = kf[h] * w
        state = lax.dot_general(
            kw.astype(BF16), vb[h], (((0,), (0,)), ((), ())), preferred_element_type=F32
        )
        n = jnp.sum(kw, axis=0, keepdims=True)
        own_n[h, 0:1, :] = n[:, :128]
        own_n[h, 1:2, :] = n[:, 128:]
        own_n[h, 2:3, :] = jnp.broadcast_to(end, (1, 128))
        own_n[h, 3:4, :] = jnp.broadcast_to(top + end, (1, 128))
        if turn == 0:
            gone[...] = state.astype(BF16)
            for c in swap:
                c.start()
        else:
            own_c[...] = state
    gather(0, 1)
    for c in swap:
        c.wait()

    mine_n, their_n = own_n[core], came_n[...]
    first = core == 0
    n0, n1 = jnp.where(first, mine_n, their_n), jnp.where(first, their_n, mine_n)
    f0, t0, f1, t1 = n0[2:3], n0[3:4], n1[2:3], n1[3:4]
    top = jnp.maximum(t0 + f1, t1)
    w0, w1 = jnp.exp(t0 + f1 - top), jnp.exp(t1 - top)
    w_mine, w_their = jnp.where(first, w0, w1), jnp.where(first, w1, w0)
    width = own_c.shape[1]
    chip_c[...] = (
        own_c[...] * wide(w_mine, width) + came[...].astype(F32) * wide(w_their, width)
    ).astype(BF16)
    chip_n[0:2, :] = n0[0:2] * w0 + n1[0:2] * w1
    chip_n[2:3, :] = f0 + f1
    chip_n[3:4, :] = top

    def to_owner(other):
        at = pl.ds(pl.multiple_of(other * part, part), part)
        who = (other * 2 + core, y)
        return (
            pltpu.make_async_remote_copy(
                src_ref=chip_n, dst_ref=slots_n.at[chip], send_sem=sns.at[other], recv_sem=rns.at[chip],
                device_id=who, device_id_type=MESH),
            pltpu.make_async_remote_copy(
                src_ref=chip_c.at[at], dst_ref=slots.at[chip], send_sem=ss.at[other], recv_sem=rs.at[chip],
                device_id=who, device_id_type=MESH),
        )

    def from_chip(other):
        who = (other * 2 + core, y)
        return (
            pltpu.make_async_remote_copy(
                src_ref=chip_n, dst_ref=slots_n.at[other], send_sem=sns.at[other], recv_sem=rns.at[other],
                device_id=who, device_id_type=MESH),
            pltpu.make_async_remote_copy(
                src_ref=chip_c.at[pl.ds(0, part)], dst_ref=slots.at[other], send_sem=ss.at[other],
                recv_sem=rs.at[other], device_id=who, device_id_type=MESH),
        )

    def send(i, _):
        for c in to_owner(lax.rem(chip + i, chips)):
            c.start()
        return 0

    lax.fori_loop(1, chips, send, 0)
    slots_n[chip] = chip_n[...]
    slots[chip] = chip_c[pl.ds(pl.multiple_of(chip * part, part), part), :]

    def attend(h):
        loads[3 * h + 2].wait()
        q = qf[h] * 0.0625
        q_hi = q.astype(BF16)
        q_lo = (q - q_hi.astype(F32)).astype(BF16)
        qf[h] = q
        qc[h, :, 0:256] = q_hi
        qc[h, :, 256:512] = q_hi
        qc[h, :, 512:768] = q_lo
        k = kf[h]
        k_hi = k.astype(BF16)
        k_lo = (k - k_hi.astype(F32)).astype(BF16)
        kc[:, 0:256] = k_hi
        kc[:, 256:512] = k_lo
        kc[:, 512:768] = k_hi
        for i in range(rows // tile):
            at = slice(i * tile, (i + 1) * tile)
            peak_col = gcol[at, 2 + h:3 + h]
            upto = (i + 1) * tile
            s = lax.dot_general(
                qc[h, at, :], kc[0:upto, :], (((1,), (1,)), ((), ())), preferred_element_type=F32
            )
            z = grow[h:h + 1, 0:upto] - peak_col
            r = lax.broadcasted_iota(jnp.int32, (tile, upto), 0) + i * tile
            c = lax.broadcasted_iota(jnp.int32, (tile, upto), 1)
            w = jnp.exp(jnp.where(c <= r, z, -jnp.inf)) * s
            den[h, at, :] = jnp.sum(w, axis=1, keepdims=True)
            num[h, at, :] = jnp.dot(w.astype(BF16), vb[h, 0:upto, :], preferred_element_type=F32)

    for f in range(2, 5):
        gather(f, 0)
    attend(0)
    gather(1, 1)
    gather(0, 2)

    def got_n(i, _):
        from_chip(lax.rem(chip + i, chips))[0].wait_recv()
        return 0

    lax.fori_loop(1, chips, got_n, 0)

    def got_c(i, _):
        from_chip(lax.rem(chip + i, chips))[1].wait_recv()
        return 0

    lax.fori_loop(1, chips, got_c, 0)

    def give_back(other):
        return pltpu.make_async_remote_copy(
            src_ref=back.at[other], dst_ref=prefix.at[pl.ds(pl.multiple_of(chip * part, part), part)],
            send_sem=sb.at[other], recv_sem=rb.at[chip], device_id=(other * 2 + core, y), device_id_type=MESH)

    def take_back(other):
        return pltpu.make_async_remote_copy(
            src_ref=back.at[other], dst_ref=prefix.at[pl.ds(pl.multiple_of(other * part, part), part)],
            send_sem=sb.at[other], recv_sem=rb.at[other], device_id=(other * 2 + core, y), device_id_type=MESH)

    def scan(p, carry):
        m, c, n = carry
        back[p] = c.astype(BF16)

        @pl.when(p == chip)
        def _():
            pre_n[0:2, :] = n
            pre_n[2:3, :] = m
            prefix[pl.ds(pl.multiple_of(chip * part, part), part), :] = c.astype(BF16)

        @pl.when(p != chip)
        def _():
            give_back(p).start()

        later = slots_n[p]
        f, t = later[2:3], later[3:4]
        top = jnp.maximum(m + f, t)
        a, b = jnp.exp(m + f - top), jnp.exp(t - top)
        c = c * wide(a, width) + slots[p].astype(F32) * wide(b, width)
        return top, c, n * a + later[0:2] * b

    lax.fori_loop(
        0, chips, scan,
        (jnp.full((1, 128), LOW, F32), jnp.zeros((part, width), F32), jnp.zeros((2, 128), F32)),
    )

    attend(1)
    gather(2, 1)

    def got_back(i, _):
        take_back(lax.rem(chip + i, chips)).wait_recv()
        return 0

    lax.fori_loop(1, chips, got_back, 0)

    gather(0, 3)
    gather(1, 2)
    pm, pn = pre_n[2:3, :], pre_n[0:2, :]
    top = jnp.maximum(pm + f0, t0)
    a, b = jnp.exp(pm + f0 - top), jnp.exp(t0 - top)
    zero = jnp.zeros_like(b)
    b_mine, b_their = jnp.where(first, b, zero), jnp.where(first, zero, b)
    p_c = prefix[...].astype(F32)
    second_c = (
        p_c * wide(a, width) + own_c[...] * wide(b_mine, width) + came[...].astype(F32) * wide(b_their, width)
    )
    second_n = pn * a + n0[0:2] * b
    fix[core] = jnp.where(first, p_c, second_c).astype(BF16)
    out_c[...] = jnp.where(first, second_c, p_c).astype(BF16)
    fix_n[core, 0:2, :] = jnp.where(first, pn, second_n)
    fix_n[core, 2:3, :] = jnp.where(first, pm, top)
    out_n[0:2, :] = jnp.where(first, second_n, pn)
    out_n[2:3, :] = jnp.where(first, top, pm)
    out_n[3:4, :] = jnp.zeros((1, 128), F32)
    tell = [
        pltpu.make_async_remote_copy(
            src_ref=out_c, dst_ref=fix.at[core], send_sem=pair_sem.at[4], recv_sem=pair_sem.at[5],
            device_id=(mate, y), device_id_type=MESH),
        pltpu.make_async_remote_copy(
            src_ref=out_n, dst_ref=fix_n.at[core], send_sem=pair_sem.at[6], recv_sem=pair_sem.at[7],
            device_id=(mate, y), device_id_type=MESH),
    ]
    for c in tell:
        c.start()
    for c in tell:
        c.wait()

    def finish(start, count):
        at = pl.ds(pl.multiple_of(start, 64), count)
        for h in range(2):
            pm = fix_n[h, 2:3, 0:1]
            n_row = jnp.concatenate([fix_n[h, 0:1, :], fix_n[h, 1:2, :]], axis=1)
            peak_col = gcol[at, 2 + h:3 + h]
            top = jnp.maximum(peak_col, pm)
            ow, iw = jnp.exp(peak_col - top), jnp.exp(pm - top)
            mem = jnp.dot(qc[h, at, 0:256], fix[h], preferred_element_type=F32)
            mem_n = jnp.sum(qf[h, at, :] * n_row, axis=1, keepdims=True)
            d = jnp.maximum(jnp.abs(ow * den[h, at, :] + iw * mem_n), 1.0)
            inv = 1.0 / d
            hidden[at, h * width:(h + 1) * width] = (
                (ow * inv) * num[h, at, :] + (iw * inv) * mem
            ).astype(BF16)

    small, count = 64, 4
    big = half - small * count

    def rows_at(mine, c):
        base = (kept if mine else 1 - kept) * half
        return base + c * small, (small if c is not count else big)

    def x_copy(c):
        start, size = rows_at(False, c)
        return pltpu.make_async_remote_copy(
            src_ref=hidden.at[pl.ds(pl.multiple_of(start, small), size)],
            dst_ref=swapped.at[pl.ds(pl.multiple_of(c * small, small), size)], send_sem=xs.at[c], recv_sem=xr.at[c],
            device_id=(ctx, partner), device_id_type=MESH)

    def small_piece(c, p):
        lo, w = ((0, block // 2), (block // 2, block // 2), (0, block))[p]
        return c, p // 2, lo, w, c * 3 + p

    def big_piece(b, j):
        w = block // 4
        return count, b, pl.multiple_of(j * w, w), w, 3 * count + b * 4 + j

    def y_copy(piece):
        c, b, lo, w, i = piece
        at = (b, pl.ds(pl.multiple_of(c * small, small), rows_at(True, c)[1]), pl.ds(lo, w))
        return pltpu.make_async_remote_copy(
            src_ref=y_out.at[at], dst_ref=y_in.at[at], send_sem=ys.at[i], recv_sem=yr.at[i],
            device_id=(ctx, across), device_id_type=MESH)

    def z_copy(piece, incoming):
        c, b, lo, w, i = piece
        start, size = rows_at(not incoming, c)
        return pltpu.make_async_remote_copy(
            src_ref=z_out.at[pl.ds(pl.multiple_of(c * small, small), size), pl.ds(lo, w)],
            dst_ref=out.at[pl.ds(pl.multiple_of(start, small), size), pl.ds(lo, w)],
            send_sem=zs.at[i], recv_sem=zr.at[i], device_id=(ctx, partner), device_id_type=MESH)

    def project(f, piece):
        c, b, lo, w, i = piece
        start, size = rows_at(True, c)
        return jnp.dot(
            hidden[pl.ds(pl.multiple_of(start, small), size), :], w_own[f, :, pl.ds(lo, w)],
            preferred_element_type=F32,
        ) + jnp.dot(
            swapped[pl.ds(pl.multiple_of(c * small, small), size), :], w_mate[f, :, pl.ds(lo, w)],
            preferred_element_type=F32,
        )

    def y_step(piece):
        c, b, lo, w, i = piece
        y_out[b, pl.ds(pl.multiple_of(c * small, small), rows_at(True, c)[1]), pl.ds(lo, w)] = project(b, piece).astype(BF16)
        y_copy(piece).start()

    def f_step(piece):
        c, b, lo, w, i = piece
        start, size = rows_at(True, c)
        mine = project(2 + b, piece)
        y_copy(piece).wait_recv()
        at = pl.ds(pl.multiple_of(c * small, small), size)
        total = (mine + y_in[b, at, pl.ds(lo, w)].astype(F32)).astype(BF16)
        if b == 0:
            z_out[at, pl.ds(lo, w)] = total
            z_copy(piece, False).start()
        else:
            out[pl.ds(pl.multiple_of(start, small), size), pl.ds(lo, w)] = total

    def each(n, body):
        def one(i, _):
            body(i)
            return 0

        lax.fori_loop(0, n, one, 0)

    def finish_chunk(mine, c):
        finish(*rows_at(mine, c))
        if not mine:
            x_copy(c).start()

    finish_chunk(False, 0)
    finish_chunk(True, 0)
    each(count - 1, lambda i: finish_chunk(False, i + 1))
    gather(2, 2)
    gather(3, 1)
    finish_chunk(False, count)
    each(count - 1, lambda i: finish_chunk(True, i + 1))
    finish_chunk(True, count)
    for c in w_loads:
        c.wait()
    gather(1, 3)
    gather(0, 4)

    def first_columns(c):
        x_copy(c).wait_recv()
        y_step(small_piece(c, 0))

        @pl.when(c == 0)
        def _():
            gather(1, 4)

        y_step(small_piece(c, 1))

        @pl.when(c == 1)
        def _():
            gather(3, 2)
            gather(4, 1)

        @pl.when(c == 2)
        def _():
            gather(2, 3)

    each(count, first_columns)
    gather(2, 4)
    each(count, lambda c: y_step(small_piece(c, 2)))
    gather(3, 3)
    gather(4, 2)
    gather(3, 4)

    def for_partner(c):
        f_step(small_piece(c, 0))
        f_step(small_piece(c, 1))

    each(count, for_partner)
    x_copy(count).wait_recv()
    each(4, lambda j: y_step(big_piece(0, j)))
    each(4, lambda j: y_step(big_piece(1, j)))
    gather(4, 3)
    gather(4, 4)
    each(count, lambda c: f_step(small_piece(c, 2)))
    each(4, lambda j: f_step(big_piece(0, j)))
    each(4, lambda j: f_step(big_piece(1, j)))

    for f in range(5):
        gather_sent(f)

    def small_done(c):
        x_copy(c).wait_send()
        for p in range(3):
            y_copy(small_piece(c, p)).wait_send()
        for p in range(2):
            z_copy(small_piece(c, p), False).wait_send()
            z_copy(small_piece(c, p), True).wait_recv()

    def big_done(j):
        y_copy(big_piece(0, j)).wait_send()
        y_copy(big_piece(1, j)).wait_send()
        z_copy(big_piece(0, j), False).wait_send()
        z_copy(big_piece(0, j), True).wait_recv()

    each(count, small_done)
    x_copy(count).wait_send()
    each(4, big_done)

    def sent(i, _):
        other = lax.rem(chip + i, chips)
        for c in to_owner(other):
            c.wait_send()
        give_back(other).wait_send()
        return 0

    lax.fori_loop(1, chips, sent, 0)


def layer(queries, keys, values, out_weight, gate_in, gate_f):
    rows, heads, dk = queries.shape
    dv = values.shape[2]
    chips = lax.axis_size("ctx") // 2
    part = dk // chips
    hbm = pl.BlockSpec(memory_space=pl.ANY)
    vmem = pl.BlockSpec(memory_space=pltpu.VMEM)
    V = pltpu.VMEM
    dma = pltpu.SemaphoreType.DMA
    return pl.pallas_call(
        layer_kernel,
        out_shape=jax.ShapeDtypeStruct((rows, out_weight.shape[1] // 4), BF16),
        in_specs=[hbm, hbm, hbm, hbm, vmem, vmem],
        out_specs=vmem,
        scratch_shapes=[
            V((heads, rows, dk), F32), V((heads, rows, dk), F32), V((heads, rows, dv), F32),
            V((heads, rows, 3 * dk), BF16), V((rows, 3 * dk), BF16), V((heads, rows, dv), BF16),
            V((heads, rows, dv), F32), V((heads, rows, 1), F32), V((rows, 8), F32), V((8, rows), F32),
            V((dk, dv), F32), V((heads, 4, 128), F32), V((dk, dv), BF16), V((4, 128), F32),
            V((dk, dv), BF16), V((4, 128), F32),
            V((dk, dv), BF16), V((4, 128), F32), V((chips, part, dv), BF16), V((chips, 4, 128), F32),
            V((chips, part, dv), BF16), V((dk, dv), BF16), V((4, 128), F32),
            V((heads, dk, dv), BF16), V((heads, 4, 128), F32), V((dk, dv), BF16), V((4, 128), F32),
            V((rows, heads * dv), BF16), V((rows // 2, heads * dv), BF16),
            V((4, heads * dv, out_weight.shape[1] // 4), BF16), V((4, heads * dv, out_weight.shape[1] // 4), BF16),
            V((2, rows // 2, out_weight.shape[1] // 4), BF16), V((2, rows // 2, out_weight.shape[1] // 4), BF16),
            V((rows // 2, out_weight.shape[1] // 4), BF16),
            dma((2, 3)), dma((4,)), dma((8,)), dma((chips,)), dma((chips,)), dma((chips,)), dma((chips,)),
            dma((chips,)), dma((chips,)),
            dma((5, 2)), dma((5, 2)), dma((5, 2, 6)), dma((5, 2, 6)), dma((5,)), dma((5,)),
            dma((5,)), dma((5,)), dma((20,)), dma((20,)), dma((20,)), dma((20,)),
        ],
        compiler_params=pltpu.CompilerParams(
            collective_id=0, has_side_effects=True, vmem_limit_bytes=60 << 20
        ),
        name="layer",
    )(queries, keys, values, out_weight, gate_in, gate_f)


def on_device(queries, keys, values, entry_gate_logit, forget_gate, out_weight):
    return layer(queries, keys, values, out_weight, entry_gate_logit, forget_gate)


def solution(mesh):
    placed = (
        P("ctx", "head", None),
        P("ctx", "head", None),
        P("ctx", "head", None),
        P("head", "ctx"),
        P("head", "ctx"),
        P("head", None),
    )
    return jax.shard_map(
        on_device, mesh=mesh, in_specs=placed, out_specs=P("ctx", "head"), check_vma=False
    )
```

```python
import functools

import jax
import jax.numpy as jnp
from jax import lax
from jax.experimental import pallas as pl
from jax.experimental.pallas import tpu as pltpu
from jax.sharding import PartitionSpec as P

MESH = pl.DeviceIdType.MESH
F32, BF16 = jnp.float32, jnp.bfloat16
LOW = -1e30


def running(x, join, fill):
    lane = lax.broadcasted_iota(jnp.int32, x.shape, 1)
    row = lax.broadcasted_iota(jnp.int32, x.shape, 0)
    for step in (1, 2, 4, 8, 16, 32, 64):
        x = join(x, jnp.where(lane >= step, pltpu.roll(x, step, 1), fill))
    ends = jnp.broadcast_to(x[:, 127:128], x.shape)
    ends = jnp.where(row >= 2, pltpu.roll(ends, 2, 0), fill)
    for step in (2, 4, 8):
        ends = join(ends, jnp.where(row >= step, pltpu.roll(ends, step, 0), fill))
    return join(x, ends)


def stacked(x):
    return jnp.concatenate([x[:, j:j + 128] for j in range(0, x.shape[1], 128)], axis=0)


def unstacked(x):
    return jnp.concatenate([x[j:j + 2, :] for j in range(0, x.shape[0], 2)], axis=1)


def log_sigmoid(x):
    e = jnp.exp(-jnp.abs(x))
    u = 1.0 + e
    tail = jnp.where(u == 1.0, e, jnp.log(u) * (e / jnp.where(u == 1.0, 1.0, u - 1.0)))
    return jnp.minimum(x, 0.0) - tail


def wide(row, width):
    return jnp.concatenate([row] * (width // row.shape[1]), axis=1)


def layer_kernel(
    q_hbm, k_hbm, v_hbm, w_hbm, in_hbm, f_hbm, out,
    gate_in, gate_f,
    qf, kf, vf, qc, kc, vb, num, den, gcol, grow, own_c, own_n, gone, gone_n, came, came_n,
    chip_c, chip_n, slots, slots_n, back, prefix, pre_n, fix, fix_n, out_c, out_n,
    hidden, swapped, w_own, w_mate, y_out, y_in, z_out,
    e_out, e_in, e_sum, e_got, e_sum2, edge_s, edge_r, edge_k, out_own, gate_sem, own_sem, load_sem, w_sem, pair_sem, ss, rs, sns, rns, sb, rb,
    fetch_s, fetch_r, ring_s, ring_r, share_s, share_r, xs, xr, ys, yr, zs, zr,
):
    rows = q_hbm.shape[0]
    tile = 256
    ctx, y = lax.axis_index("ctx"), lax.axis_index("head")
    core = lax.rem(ctx, 2)
    chip = lax.div(ctx, 2)
    mate = ctx + 1 - 2 * core
    chips = slots.shape[0]
    part = slots.shape[1]
    side = lax.rem(y, 2)
    pair = lax.div(y, 2)
    partner = y + 1 - 2 * side
    across = 3 - y
    kept = lax.rem(lax.div(y + 1, 2), 2)
    cx, cz = lax.rem(chip, 4), lax.div(chip, 4)
    half = rows // 2
    block = w_own.shape[2]

    def column(b, part_of, of_y):
        other = of_y + 1 - 2 * part_of
        start = (lax.div(of_y, 2) * -2 + 2 + part_of, lax.div(of_y, 2) * -2 + 3 - part_of, other, of_y)[b]
        return start * block

    gates = [
        pltpu.make_async_copy(f_hbm, gate_f, gate_sem.at[0]),
        pltpu.make_async_copy(in_hbm, gate_in, gate_sem.at[1]),
    ]
    for c in gates:
        c.start()
    loads = []
    for h in range(2):
        for j, (src, dst) in enumerate(((k_hbm, kf), (v_hbm, vf), (q_hbm, qf))):
            loads.append(pltpu.make_async_copy(src.at[:, h, :], dst.at[h], load_sem.at[h, j]))
    for c in (0, 1, 3, 4, 2, 5):
        loads[c].start()
    barrier = pltpu.get_barrier_semaphore()
    for who in ((mate, y), (ctx, partner), (ctx, across)):
        pl.semaphore_signal(barrier, inc=1, device_id=who, device_id_type=MESH)

    def greet(i, _):
        other = lax.rem(chip + i, chips) * 2 + core
        pl.semaphore_signal(barrier, inc=1, device_id=(other, y), device_id_type=MESH)
        return 0

    lax.fori_loop(1, chips, greet, 0)

    w_loads = [
        pltpu.make_async_copy(
            w_hbm.at[:, pl.ds(pl.multiple_of(column(b, side, y), block), block)], w_own.at[b], w_sem.at[b])
        for b in range(4)
    ]

    parts = ((0, 0, block // 2), (0, block // 2, block // 2), (1, 0, block), (2, 0, block), (3, 0, block))

    def strip(f, path, z_at, x_at, count):
        at = z_at * 4 + x_at if path == 0 else x_at * 4 + z_at
        b, lo, width = parts[f]
        return w_mate.at[
            b, pl.ds(pl.multiple_of((core * 2 + path) * 256 + at * 16, 16), 16 * count), pl.ds(lo, width)]

    def fetch(f, path):
        at = cz * 4 + cx if path == 0 else cx * 4 + cz
        b, lo, width = parts[f]
        col = column(b, 1 - side, partner) + lo
        return pltpu.make_async_remote_copy(
            src_ref=w_hbm.at[
                pl.ds(pl.multiple_of((core * 2 + path) * 256 + at * 16, 16), 16),
                pl.ds(pl.multiple_of(col, 128), width)],
            dst_ref=strip(f, path, cz, cx, 1),
            send_sem=fetch_s.at[f, path], recv_sem=fetch_r.at[f, path], device_id=(ctx, partner), device_id_type=MESH)

    def spread(f, path, stage, way, incoming):
        along_x = (path == 0) == (stage == 0)
        here = cx if along_x else cz
        to = lax.rem(here + way, 4)
        owner = lax.rem(here + 4 - way, 4) if incoming else here
        if stage == 0:
            ref = strip(f, path, cz, owner, 1) if along_x else strip(f, path, owner, cx, 1)
        else:
            ref = strip(f, path, 0, owner, 4) if along_x else strip(f, path, owner, 0, 4)
        peer = (cz * 4 + to if along_x else to * 4 + cx) * 2 + core
        i = stage * 3 + way - 1
        return pltpu.make_async_remote_copy(
            src_ref=ref, dst_ref=ref, send_sem=ring_s.at[f, path, i], recv_sem=ring_r.at[f, path, i],
            device_id=(peer, y), device_id_type=MESH)

    def share(f, who):
        b, lo, width = parts[f]
        ref = w_mate.at[b, pl.ds(pl.multiple_of(who * 512, 512), 512), pl.ds(lo, width)]
        return pltpu.make_async_remote_copy(
            src_ref=ref, dst_ref=ref, send_sem=share_s.at[f], recv_sem=share_r.at[f],
            device_id=(mate, y), device_id_type=MESH)

    def gather(f, *steps):
        for step in steps:
            for path in range(2):
                if step == 0:
                    fetch(f, path).start()
                if step == 1:
                    fetch(f, path).wait_recv()
                for way in (1, 3, 2):
                    if step == 2 or step == 3:
                        spread(f, path, step - 2, way, True).wait_recv()
                for way in (1, 3, 2):
                    if step == 1 or step == 2:
                        spread(f, path, step - 1, way, False).start()
            if step == 3:
                share(f, core).start()
            if step == 4:
                share(f, 1 - core).wait_recv()

    def gather_sent(f):
        for path in range(2):
            fetch(f, path).wait_send()
            for i in range(6):
                spread(f, path, i // 3, i % 3 + 1, False).wait_send()
        share(f, core).wait_send()

    for c in gates:
        c.wait()
    cum = running(log_sigmoid(stacked(gate_f[...])), jnp.add, 0.0)
    g = stacked(gate_in[...]) - cum
    peak = running(g, jnp.maximum, LOW)
    f_end = cum[14:16, 127:128]
    g_top = peak[14:16, 127:128]
    g, peak = unstacked(g), unstacked(peak)
    grow[0:2, :] = g
    gcol[...] = jnp.transpose(jnp.concatenate([g, peak, g, peak], axis=0), (1, 0))
    pl.semaphore_wait(barrier, chips + 2)
    gather(0, 0)
    gather(1, 0)
    for c in (0, 1, 3, 4):
        loads[c].wait()
    swap = [
        pltpu.make_async_remote_copy(
            src_ref=gone, dst_ref=came, send_sem=pair_sem.at[0], recv_sem=pair_sem.at[1],
            device_id=(mate, y), device_id_type=MESH),
        pltpu.make_async_remote_copy(
            src_ref=own_n.at[1 - core], dst_ref=came_n, send_sem=pair_sem.at[2], recv_sem=pair_sem.at[3],
            device_id=(mate, y), device_id_type=MESH),
    ]
    for turn, h in enumerate((1 - core, core)):
        lead = h == 0
        vb[h] = vf[h].astype(BF16)
        top = jnp.where(lead, g_top[0:1, :], g_top[1:2, :])
        end = jnp.where(lead, f_end[0:1, :], f_end[1:2, :])
        w = jnp.exp(jnp.where(lead, gcol[:, 0:1], gcol[:, 1:2]) - top)
        kw = kf[h] * w
        state = lax.dot_general(
            kw.astype(BF16), vb[h], (((0,), (0,)), ((), ())), preferred_element_type=F32
        )
        n = jnp.sum(kw, axis=0, keepdims=True)
        own_n[h, 0:1, :] = n[:, :128]
        own_n[h, 1:2, :] = n[:, 128:]
        own_n[h, 2:3, :] = jnp.broadcast_to(end, (1, 128))
        own_n[h, 3:4, :] = jnp.broadcast_to(top + end, (1, 128))
        if turn == 0:
            gone[...] = state.astype(BF16)
            for c in swap:
                c.start()
        else:
            own_c[...] = state
    gather(0, 1)
    for c in swap:
        c.wait()

    mine_n, their_n = own_n[core], came_n[...]
    first = core == 0
    n0, n1 = jnp.where(first, mine_n, their_n), jnp.where(first, their_n, mine_n)
    f0, t0, f1, t1 = n0[2:3], n0[3:4], n1[2:3], n1[3:4]
    top = jnp.maximum(t0 + f1, t1)
    w0, w1 = jnp.exp(t0 + f1 - top), jnp.exp(t1 - top)
    w_mine, w_their = jnp.where(first, w0, w1), jnp.where(first, w1, w0)
    width = own_c.shape[1]
    chip_c[...] = (
        own_c[...] * wide(w_mine, width) + came[...].astype(F32) * wide(w_their, width)
    ).astype(BF16)
    chip_n[0:2, :] = n0[0:2] * w0 + n1[0:2] * w1
    chip_n[2:3, :] = f0 + f1
    chip_n[3:4, :] = top

    def to_owner(other):
        at = pl.ds(pl.multiple_of(other * part, part), part)
        who = (other * 2 + core, y)
        return (
            pltpu.make_async_remote_copy(
                src_ref=chip_n, dst_ref=slots_n.at[chip], send_sem=sns.at[other], recv_sem=rns.at[chip],
                device_id=who, device_id_type=MESH),
            pltpu.make_async_remote_copy(
                src_ref=chip_c.at[at], dst_ref=slots.at[chip], send_sem=ss.at[other], recv_sem=rs.at[chip],
                device_id=who, device_id_type=MESH),
        )

    def from_chip(other):
        who = (other * 2 + core, y)
        return (
            pltpu.make_async_remote_copy(
                src_ref=chip_n, dst_ref=slots_n.at[other], send_sem=sns.at[other], recv_sem=rns.at[other],
                device_id=who, device_id_type=MESH),
            pltpu.make_async_remote_copy(
                src_ref=chip_c.at[pl.ds(0, part)], dst_ref=slots.at[other], send_sem=ss.at[other],
                recv_sem=rs.at[other], device_id=who, device_id_type=MESH),
        )

    def send(i, _):
        for c in to_owner(lax.rem(chip + i, chips)):
            c.start()
        return 0

    lax.fori_loop(1, chips, send, 0)
    slots_n[chip] = chip_n[...]
    slots[chip] = chip_c[pl.ds(pl.multiple_of(chip * part, part), part), :]

    def attend(h):
        loads[3 * h + 2].wait()
        q = qf[h] * 0.0625
        q_hi = q.astype(BF16)
        q_lo = (q - q_hi.astype(F32)).astype(BF16)
        qf[h] = q
        qc[h, :, 0:256] = q_hi
        qc[h, :, 256:512] = q_hi
        qc[h, :, 512:768] = q_lo
        k = kf[h]
        k_hi = k.astype(BF16)
        k_lo = (k - k_hi.astype(F32)).astype(BF16)
        kc[:, 0:256] = k_hi
        kc[:, 256:512] = k_lo
        kc[:, 512:768] = k_hi
        for i in range(rows // tile):
            at = slice(i * tile, (i + 1) * tile)
            peak_col = gcol[at, 2 + h:3 + h]
            upto = (i + 1) * tile
            s = lax.dot_general(
                qc[h, at, :], kc[0:upto, :], (((1,), (1,)), ((), ())), preferred_element_type=F32
            )
            z = grow[h:h + 1, 0:upto] - peak_col
            r = lax.broadcasted_iota(jnp.int32, (tile, upto), 0) + i * tile
            c = lax.broadcasted_iota(jnp.int32, (tile, upto), 1)
            w = jnp.exp(jnp.where(c <= r, z, -jnp.inf)) * s
            den[h, at, :] = jnp.sum(w, axis=1, keepdims=True)
            num[h, at, :] = jnp.dot(w.astype(BF16), vb[h, 0:upto, :], preferred_element_type=F32)

    for f in range(2, 5):
        gather(f, 0)
    for c in w_loads:
        c.start()
    attend(0)
    gather(1, 1)
    gather(0, 2)

    def got_n(i, _):
        from_chip(lax.rem(chip + i, chips))[0].wait_recv()
        return 0

    lax.fori_loop(1, chips, got_n, 0)

    def got_c(i, _):
        from_chip(lax.rem(chip + i, chips))[1].wait_recv()
        return 0

    lax.fori_loop(1, chips, got_c, 0)

    def give_back(other):
        return pltpu.make_async_remote_copy(
            src_ref=back.at[other], dst_ref=prefix.at[pl.ds(pl.multiple_of(chip * part, part), part)],
            send_sem=sb.at[other], recv_sem=rb.at[chip], device_id=(other * 2 + core, y), device_id_type=MESH)

    def take_back(other):
        return pltpu.make_async_remote_copy(
            src_ref=back.at[other], dst_ref=prefix.at[pl.ds(pl.multiple_of(other * part, part), part)],
            send_sem=sb.at[other], recv_sem=rb.at[other], device_id=(other * 2 + core, y), device_id_type=MESH)

    def scan(p, carry):
        m, c, n = carry
        back[p] = c.astype(BF16)

        @pl.when(p == chip)
        def _():
            pre_n[0:2, :] = n
            pre_n[2:3, :] = m
            prefix[pl.ds(pl.multiple_of(chip * part, part), part), :] = c.astype(BF16)

        @pl.when(p != chip)
        def _():
            give_back(p).start()

        later = slots_n[p]
        f, t = later[2:3], later[3:4]
        top = jnp.maximum(m + f, t)
        a, b = jnp.exp(m + f - top), jnp.exp(t - top)
        c = c * wide(a, width) + slots[p].astype(F32) * wide(b, width)
        return top, c, n * a + later[0:2] * b

    lax.fori_loop(
        0, chips, scan,
        (jnp.full((1, 128), LOW, F32), jnp.zeros((part, width), F32), jnp.zeros((2, 128), F32)),
    )

    attend(1)
    gather(2, 1)

    def got_back(i, _):
        take_back(lax.rem(chip + i, chips)).wait_recv()
        return 0

    lax.fori_loop(1, chips, got_back, 0)

    gather(0, 3)
    gather(1, 2)
    gather(3, 1)
    pm, pn = pre_n[2:3, :], pre_n[0:2, :]
    top = jnp.maximum(pm + f0, t0)
    a, b = jnp.exp(pm + f0 - top), jnp.exp(t0 - top)
    zero = jnp.zeros_like(b)
    b_mine, b_their = jnp.where(first, b, zero), jnp.where(first, zero, b)
    p_c = prefix[...].astype(F32)
    second_c = (
        p_c * wide(a, width) + own_c[...] * wide(b_mine, width) + came[...].astype(F32) * wide(b_their, width)
    )
    second_n = pn * a + n0[0:2] * b
    fix[core] = jnp.where(first, p_c, second_c).astype(BF16)
    out_c[...] = jnp.where(first, second_c, p_c).astype(BF16)
    fix_n[core, 0:2, :] = jnp.where(first, pn, second_n)
    fix_n[core, 2:3, :] = jnp.where(first, pm, top)
    out_n[0:2, :] = jnp.where(first, second_n, pn)
    out_n[2:3, :] = jnp.where(first, top, pm)
    out_n[3:4, :] = jnp.zeros((1, 128), F32)
    tell = [
        pltpu.make_async_remote_copy(
            src_ref=out_c, dst_ref=fix.at[core], send_sem=pair_sem.at[4], recv_sem=pair_sem.at[5],
            device_id=(mate, y), device_id_type=MESH),
        pltpu.make_async_remote_copy(
            src_ref=out_n, dst_ref=fix_n.at[core], send_sem=pair_sem.at[6], recv_sem=pair_sem.at[7],
            device_id=(mate, y), device_id_type=MESH),
    ]
    for c in tell:
        c.start()

    def finish_head(start, size, h):
        at = pl.ds(pl.multiple_of(start, 32), size)
        pm = fix_n[h, 2:3, 0:1]
        n_row = jnp.concatenate([fix_n[h, 0:1, :], fix_n[h, 1:2, :]], axis=1)
        peak_col = jnp.where(h == 0, gcol[at, 2:3], gcol[at, 3:4])
        top = jnp.maximum(peak_col, pm)
        ow, iw = jnp.exp(peak_col - top), jnp.exp(pm - top)
        mem = jnp.dot(qc[h, at, 0:256], fix[h], preferred_element_type=F32)
        mem_n = jnp.sum(qf[h, at, :] * n_row, axis=1, keepdims=True)
        d = jnp.maximum(jnp.abs(ow * den[h, at, :] + iw * mem_n), 1.0)
        inv = 1.0 / d
        hidden[at, pl.ds(pl.multiple_of(h * width, width), width)] = (
            (ow * inv) * num[h, at, :] + (iw * inv) * mem
        ).astype(BF16)

    def finish(start, size):
        finish_head(start, size, 1 - core)

    def ready_head(i, _):
        finish_head(i * tile, tile, core)
        return 0

    lax.fori_loop(0, rows // tile, ready_head, 0)
    for c in tell:
        c.wait()


    edge, small, count = 32, 64, 4
    big = half - edge - small * count

    def rows_at(mine, c):
        base = (kept if mine else 1 - kept) * half + edge
        return base + c * small, (small if c is not count else big)

    def x_copy(c):
        start, size = rows_at(False, c)
        return pltpu.make_async_remote_copy(
            src_ref=hidden.at[pl.ds(pl.multiple_of(start, edge), size)],
            dst_ref=swapped.at[pl.ds(pl.multiple_of(c * small, small), size)], send_sem=xs.at[c], recv_sem=xr.at[c],
            device_id=(ctx, partner), device_id_type=MESH)

    def small_piece(c, p):
        lo, w = ((0, block // 2), (block // 2, block // 2), (0, block))[p]
        return c, p // 2, lo, w, c * 3 + p

    def big_piece(b, j):
        w = block // 4
        return count, b, pl.multiple_of(j * w, w), w, 3 * count + b * 4 + j

    def y_copy(piece):
        c, b, lo, w, i = piece
        at = (b, pl.ds(pl.multiple_of(c * small, small), rows_at(True, c)[1]), pl.ds(lo, w))
        return pltpu.make_async_remote_copy(
            src_ref=y_out.at[at], dst_ref=y_in.at[at], send_sem=ys.at[i], recv_sem=yr.at[i],
            device_id=(ctx, across), device_id_type=MESH)

    def z_copy(piece, incoming):
        c, b, lo, w, i = piece
        start, size = rows_at(not incoming, c)
        return pltpu.make_async_remote_copy(
            src_ref=z_out.at[pl.ds(pl.multiple_of(c * small, small), size), pl.ds(lo, w)],
            dst_ref=out.at[pl.ds(pl.multiple_of(start, edge), size), pl.ds(lo, w)],
            send_sem=zs.at[i], recv_sem=zr.at[i], device_id=(ctx, partner), device_id_type=MESH)

    def project(f, piece):
        c, b, lo, w, i = piece
        start, size = rows_at(True, c)
        return jnp.dot(
            hidden[pl.ds(pl.multiple_of(start, edge), size), :], w_own[f, :, pl.ds(lo, w)],
            preferred_element_type=F32,
        ) + jnp.dot(
            swapped[pl.ds(pl.multiple_of(c * small, small), size), :], w_mate[f, :, pl.ds(lo, w)],
            preferred_element_type=F32,
        )

    def y_step(piece):
        c, b, lo, w, i = piece
        y_out[b, pl.ds(pl.multiple_of(c * small, small), rows_at(True, c)[1]), pl.ds(lo, w)] = project(b, piece).astype(BF16)
        y_copy(piece).start()

    def keep(piece):
        c, b, lo, w, i = piece
        start, size = rows_at(True, c)
        return pltpu.make_async_copy(
            out_own.at[pl.ds(pl.multiple_of(c * small, small), size), pl.ds(lo, w)],
            out.at[pl.ds(pl.multiple_of(start, edge), size), pl.ds(lo, w)], own_sem.at[i])

    def f_step(piece):
        c, b, lo, w, i = piece
        start, size = rows_at(True, c)
        mine = project(2 + b, piece)
        y_copy(piece).wait_recv()
        at = pl.ds(pl.multiple_of(c * small, small), size)
        total = (mine + y_in[b, at, pl.ds(lo, w)].astype(F32)).astype(BF16)
        if b == 0:
            z_out[at, pl.ds(lo, w)] = total
            z_copy(piece, False).start()
        else:
            out_own[at, pl.ds(lo, w)] = total
            keep(piece).start()

    def each(n, body):
        def one(i, _):
            body(i)
            return 0

        lax.fori_loop(0, n, one, 0)

    def finish_chunk(mine, c):
        finish(*rows_at(mine, c))
        if not mine:
            x_copy(c).start()

    ends = (0, half)

    def edge_rows():
        return jnp.concatenate([hidden[pl.ds(e, edge), :] for e in ends], axis=0)

    def edge_copy(b):
        return pltpu.make_async_remote_copy(
            src_ref=e_out.at[b], dst_ref=e_in.at[b], send_sem=edge_s.at[b], recv_sem=edge_r.at[b],
            device_id=(ctx, across), device_id_type=MESH)

    def edge_sum():
        return pltpu.make_async_remote_copy(
            src_ref=e_sum, dst_ref=e_got, send_sem=edge_s.at[2], recv_sem=edge_r.at[2],
            device_id=(ctx, partner), device_id_type=MESH)

    def edge_keep(i):
        return pltpu.make_async_copy(
            e_sum2.at[pl.ds(i * edge, edge)], out.at[pl.ds(ends[i], edge)], edge_k.at[i])

    finish_chunk(False, 0)
    for e in ends:
        finish(e, edge)
    for b in range(2):
        w_loads[b].wait()
        e_out[b] = jnp.dot(edge_rows(), w_own[b], preferred_element_type=F32).astype(BF16)
        edge_copy(b).start()
    finish_chunk(True, 0)
    each(count - 1, lambda i: finish_chunk(False, i + 1))
    gather(2, 2)
    gather(4, 1)
    finish_chunk(False, count)
    each(count - 1, lambda i: finish_chunk(True, i + 1))
    finish_chunk(True, count)
    w_loads[2].wait()
    w_loads[3].wait()
    gather(1, 3)
    gather(0, 4)

    def first_columns(c):
        x_copy(c).wait_recv()
        y_step(small_piece(c, 0))

        @pl.when(c == 0)
        def _():
            gather(1, 4)
            gather(3, 2)

        y_step(small_piece(c, 1))

        @pl.when(c == 2)
        def _():
            gather(2, 3)
            gather(4, 2)

    each(count, first_columns)
    edge_copy(0).wait_recv()
    e_sum[...] = (
        jnp.dot(edge_rows(), w_own[2], preferred_element_type=F32) + e_in[0].astype(F32)).astype(BF16)
    edge_sum().start()
    gather(2, 4)
    each(count, lambda c: y_step(small_piece(c, 2)))
    gather(3, 3)
    gather(3, 4)

    def for_partner(c):
        f_step(small_piece(c, 0))
        f_step(small_piece(c, 1))

    each(count, for_partner)
    edge_copy(1).wait_recv()
    own_edge = jnp.dot(edge_rows(), w_own[3], preferred_element_type=F32) + e_in[1].astype(F32)
    edge_sum().wait_recv()
    e_sum2[...] = (own_edge + e_got[...].astype(F32)).astype(BF16)
    for i in range(2):
        edge_keep(i).start()
    x_copy(count).wait_recv()
    each(4, lambda j: y_step(big_piece(0, j)))
    each(4, lambda j: y_step(big_piece(1, j)))
    gather(4, 3)
    gather(4, 4)
    each(count, lambda c: f_step(small_piece(c, 2)))
    each(4, lambda j: f_step(big_piece(0, j)))
    each(4, lambda j: f_step(big_piece(1, j)))

    for f in range(5):
        gather_sent(f)
    edge_sum().wait_send()
    for i in range(2):
        edge_copy(i).wait_send()
        edge_keep(i).wait()

    def small_done(c):
        x_copy(c).wait_send()
        keep(small_piece(c, 2)).wait()
        for p in range(3):
            y_copy(small_piece(c, p)).wait_send()
        for p in range(2):
            z_copy(small_piece(c, p), False).wait_send()
            z_copy(small_piece(c, p), True).wait_recv()

    def big_done(j):
        y_copy(big_piece(0, j)).wait_send()
        y_copy(big_piece(1, j)).wait_send()
        keep(big_piece(1, j)).wait()
        z_copy(big_piece(0, j), False).wait_send()
        z_copy(big_piece(0, j), True).wait_recv()

    each(count, small_done)
    x_copy(count).wait_send()
    each(4, big_done)

    def sent(i, _):
        other = lax.rem(chip + i, chips)
        for c in to_owner(other):
            c.wait_send()
        give_back(other).wait_send()
        return 0

    lax.fori_loop(1, chips, sent, 0)


def layer(queries, keys, values, out_weight, gate_in, gate_f):
    rows, heads, dk = queries.shape
    dv = values.shape[2]
    chips = lax.axis_size("ctx") // 2
    part = dk // chips
    hbm = pl.BlockSpec(memory_space=pl.ANY)
    V = pltpu.VMEM
    dma = pltpu.SemaphoreType.DMA
    return pl.pallas_call(
        layer_kernel,
        out_shape=jax.ShapeDtypeStruct((rows, out_weight.shape[1] // 4), BF16),
        in_specs=[hbm] * 6,
        out_specs=hbm,
        scratch_shapes=[
            V((heads, rows), F32), V((heads, rows), F32),
            V((heads, rows, dk), F32), V((heads, rows, dk), F32), V((heads, rows, dv), F32),
            V((heads, rows, 3 * dk), BF16), V((rows, 3 * dk), BF16), V((heads, rows, dv), BF16),
            V((heads, rows, dv), F32), V((heads, rows, 1), F32), V((rows, 8), F32), V((8, rows), F32),
            V((dk, dv), F32), V((heads, 4, 128), F32), V((dk, dv), BF16), V((4, 128), F32),
            V((dk, dv), BF16), V((4, 128), F32),
            V((dk, dv), BF16), V((4, 128), F32), V((chips, part, dv), BF16), V((chips, 4, 128), F32),
            V((chips, part, dv), BF16), V((dk, dv), BF16), V((4, 128), F32),
            V((heads, dk, dv), BF16), V((heads, 4, 128), F32), V((dk, dv), BF16), V((4, 128), F32),
            V((rows, heads * dv), BF16), V((rows // 2, heads * dv), BF16),
            V((4, heads * dv, out_weight.shape[1] // 4), BF16), V((4, heads * dv, out_weight.shape[1] // 4), BF16),
            V((2, rows // 2, out_weight.shape[1] // 4), BF16), V((2, rows // 2, out_weight.shape[1] // 4), BF16),
            V((rows // 2, out_weight.shape[1] // 4), BF16),
            V((2, 64, out_weight.shape[1] // 4), BF16), V((2, 64, out_weight.shape[1] // 4), BF16),
            V((64, out_weight.shape[1] // 4), BF16), V((64, out_weight.shape[1] // 4), BF16),
            V((64, out_weight.shape[1] // 4), BF16), dma((3,)), dma((3,)), dma((2,)),
            V((rows // 2, out_weight.shape[1] // 4), BF16), dma((2,)), dma((20,)), dma((2, 3)), dma((4,)), dma((8,)), dma((chips,)), dma((chips,)), dma((chips,)), dma((chips,)),
            dma((chips,)), dma((chips,)),
            dma((5, 2)), dma((5, 2)), dma((5, 2, 6)), dma((5, 2, 6)), dma((5,)), dma((5,)),
            dma((5,)), dma((5,)), dma((20,)), dma((20,)), dma((20,)), dma((20,)),
        ],
        compiler_params=pltpu.CompilerParams(
            collective_id=0, has_side_effects=True, vmem_limit_bytes=60 << 20
        ),
        name="layer",
    )(queries, keys, values, out_weight, gate_in, gate_f)


def hand_kernel(src, dst, held, in_sem, out_sem):
    count = in_sem.shape[0]
    size = src.shape[0] // count
    at = [pl.ds(i * size, size) for i in range(count)]
    take = [pltpu.make_async_copy(src.at[a], held.at[a], in_sem.at[i]) for i, a in enumerate(at)]
    give = [pltpu.make_async_copy(held.at[a], dst.at[a], out_sem.at[i]) for i, a in enumerate(at)]
    for c in take:
        c.start()
    for c, d in zip(take, give):
        c.wait()
        d.start()
    for d in give:
        d.wait()


def handed_on(x):
    hbm = pl.BlockSpec(memory_space=pl.ANY)
    return pl.pallas_call(
        hand_kernel,
        out_shape=jax.ShapeDtypeStruct(x.shape, x.dtype),
        in_specs=[hbm],
        out_specs=hbm,
        scratch_shapes=[pltpu.VMEM(x.shape, x.dtype), pltpu.SemaphoreType.DMA((8,)), pltpu.SemaphoreType.DMA((8,))],
        name="hand_on",
    )(x)


def on_device(queries, keys, values, entry_gate_logit, forget_gate, out_weight):
    return handed_on(layer(queries, keys, values, out_weight, entry_gate_logit, forget_gate))


def solution(mesh):
    placed = (
        P("ctx", "head", None),
        P("ctx", "head", None),
        P("ctx", "head", None),
        P("head", "ctx"),
        P("head", "ctx"),
        P("head", None),
    )
    return jax.shard_map(
        on_device, mesh=mesh, in_specs=placed, out_specs=P("ctx", "head"), check_vma=False
    )
```

```python
import functools

import jax
import jax.numpy as jnp
from jax import lax
from jax.experimental import pallas as pl
from jax.experimental.pallas import tpu as pltpu
from jax.sharding import PartitionSpec as P

MESH = pl.DeviceIdType.MESH
F32, BF16 = jnp.float32, jnp.bfloat16
LOW = -1e30


def running(x, join, fill):
    lane = lax.broadcasted_iota(jnp.int32, x.shape, 1)
    row = lax.broadcasted_iota(jnp.int32, x.shape, 0)
    for step in (1, 2, 4, 8, 16, 32, 64):
        x = join(x, jnp.where(lane >= step, pltpu.roll(x, step, 1), fill))
    ends = jnp.broadcast_to(x[:, 127:128], x.shape)
    ends = jnp.where(row >= 2, pltpu.roll(ends, 2, 0), fill)
    for step in (2, 4, 8):
        ends = join(ends, jnp.where(row >= step, pltpu.roll(ends, step, 0), fill))
    return join(x, ends)


def stacked(x):
    return jnp.concatenate([x[:, j:j + 128] for j in range(0, x.shape[1], 128)], axis=0)


def unstacked(x):
    return jnp.concatenate([x[j:j + 2, :] for j in range(0, x.shape[0], 2)], axis=1)


def log_sigmoid(x):
    e = jnp.exp(-jnp.abs(x))
    u = 1.0 + e
    tail = jnp.where(u == 1.0, e, jnp.log(u) * (e / jnp.where(u == 1.0, 1.0, u - 1.0)))
    return jnp.minimum(x, 0.0) - tail


def wide(row, width):
    return jnp.concatenate([row] * (width // row.shape[1]), axis=1)


def layer_kernel(
    q_hbm, k_hbm, v_hbm, w_hbm, in_hbm, f_hbm, out,
    gate_in, gate_f,
    qf, kf, vf, qc, kc, vb, num, den, gcol, grow, own_c, own_n, gone, gone_n, came, came_n,
    chip_c, chip_n, slots, slots_n, back, prefix, pre_n, fix, fix_n, out_c, out_n,
    hidden, swapped, w_own, w_mate, y_out, y_in, z_out,
    weigh, e_out, e_in, e_sum, e_got, e_sum2, edge_s, edge_r, edge_k, out_own, gate_sem, own_sem, load_sem, w_sem, pair_sem, ss, rs, sns, rns, sb, rb,
    fetch_s, fetch_r, ring_s, ring_r, share_s, share_r, xs, xr, ys, yr, zs, zr,
):
    rows = q_hbm.shape[0]
    tile = 256
    ctx, y = lax.axis_index("ctx"), lax.axis_index("head")
    core = lax.rem(ctx, 2)
    chip = lax.div(ctx, 2)
    mate = ctx + 1 - 2 * core
    chips = slots.shape[0]
    part = slots.shape[1]
    side = lax.rem(y, 2)
    pair = lax.div(y, 2)
    partner = y + 1 - 2 * side
    across = 3 - y
    kept = lax.rem(lax.div(y + 1, 2), 2)
    cx, cz = lax.rem(chip, 4), lax.div(chip, 4)
    half = rows // 2
    block = w_own.shape[2]

    def column(b, part_of, of_y):
        other = of_y + 1 - 2 * part_of
        start = (lax.div(of_y, 2) * -2 + 2 + part_of, lax.div(of_y, 2) * -2 + 3 - part_of, other, of_y)[b]
        return start * block

    barrier = pltpu.get_barrier_semaphore()
    for who in ((mate, y), (ctx, partner), (ctx, across)):
        pl.semaphore_signal(barrier, inc=1, device_id=who, device_id_type=MESH)

    for i in range(1, chips):
        other = lax.rem(chip + i, chips) * 2 + core
        pl.semaphore_signal(barrier, inc=1, device_id=(other, y), device_id_type=MESH)

    gates = [
        pltpu.make_async_copy(f_hbm, gate_f, gate_sem.at[0]),
        pltpu.make_async_copy(in_hbm, gate_in, gate_sem.at[1]),
    ]
    for c in gates:
        c.start()
    loads = []
    for h in range(2):
        for j, (src, dst) in enumerate(((k_hbm, kf), (v_hbm, vf), (q_hbm, qf))):
            loads.append(pltpu.make_async_copy(src.at[:, h, :], dst.at[h], load_sem.at[h, j]))
    for c in (0, 1, 3, 4, 2, 5):
        loads[c].start()
    w_loads = [
        pltpu.make_async_copy(
            w_hbm.at[:, pl.ds(pl.multiple_of(column(b, side, y), block), block)], w_own.at[b], w_sem.at[b])
        for b in range(4)
    ]

    parts = ((0, 0, block // 2), (0, block // 2, block // 2), (1, 0, block), (2, 0, block), (3, 0, block))

    def strip(f, path, z_at, x_at, count):
        at = z_at * 4 + x_at if path == 0 else x_at * 4 + z_at
        b, lo, width = parts[f]
        return w_mate.at[
            b, pl.ds(pl.multiple_of((core * 2 + path) * 256 + at * 16, 16), 16 * count), pl.ds(lo, width)]

    def fetch(f, path):
        at = cz * 4 + cx if path == 0 else cx * 4 + cz
        b, lo, width = parts[f]
        col = column(b, 1 - side, partner) + lo
        return pltpu.make_async_remote_copy(
            src_ref=w_hbm.at[
                pl.ds(pl.multiple_of((core * 2 + path) * 256 + at * 16, 16), 16),
                pl.ds(pl.multiple_of(col, 128), width)],
            dst_ref=strip(f, path, cz, cx, 1),
            send_sem=fetch_s.at[f, path], recv_sem=fetch_r.at[f, path], device_id=(ctx, partner), device_id_type=MESH)

    def spread(f, path, stage, way, incoming):
        along_x = (path == 0) == (stage == 0)
        here = cx if along_x else cz
        to = lax.rem(here + way, 4)
        owner = lax.rem(here + 4 - way, 4) if incoming else here
        if stage == 0:
            ref = strip(f, path, cz, owner, 1) if along_x else strip(f, path, owner, cx, 1)
        else:
            ref = strip(f, path, 0, owner, 4) if along_x else strip(f, path, owner, 0, 4)
        peer = (cz * 4 + to if along_x else to * 4 + cx) * 2 + core
        i = stage * 3 + way - 1
        return pltpu.make_async_remote_copy(
            src_ref=ref, dst_ref=ref, send_sem=ring_s.at[f, path, i], recv_sem=ring_r.at[f, path, i],
            device_id=(peer, y), device_id_type=MESH)

    def share(f, who):
        b, lo, width = parts[f]
        ref = w_mate.at[b, pl.ds(pl.multiple_of(who * 512, 512), 512), pl.ds(lo, width)]
        return pltpu.make_async_remote_copy(
            src_ref=ref, dst_ref=ref, send_sem=share_s.at[f], recv_sem=share_r.at[f],
            device_id=(mate, y), device_id_type=MESH)

    def gather(f, *steps):
        for step in steps:
            for path in range(2):
                if step == 0:
                    fetch(f, path).start()
                if step == 1:
                    fetch(f, path).wait_recv()
                for way in (1, 3, 2):
                    if step == 2 or step == 3:
                        spread(f, path, step - 2, way, True).wait_recv()
                for way in (1, 3, 2):
                    if step == 1 or step == 2:
                        spread(f, path, step - 1, way, False).start()
            if step == 3:
                share(f, core).start()
            if step == 4:
                share(f, 1 - core).wait_recv()

    def gather_sent(f):
        for path in range(2):
            fetch(f, path).wait_send()
            for i in range(6):
                spread(f, path, i // 3, i % 3 + 1, False).wait_send()
        share(f, core).wait_send()

    for c in gates:
        c.wait()
    cum = running(log_sigmoid(stacked(gate_f[...])), jnp.add, 0.0)
    g = stacked(gate_in[...]) - cum
    peak = running(g, jnp.maximum, LOW)
    f_end = cum[14:16, 127:128]
    g_top = peak[14:16, 127:128]
    g, peak = unstacked(g), unstacked(peak)
    grow[0:2, :] = g
    gcol[...] = jnp.transpose(jnp.concatenate([g, peak, g, peak], axis=0), (1, 0))
    for c in (0, 1, 3, 4):
        loads[c].wait()
    swap = [
        pltpu.make_async_remote_copy(
            src_ref=gone, dst_ref=came, send_sem=pair_sem.at[0], recv_sem=pair_sem.at[1],
            device_id=(mate, y), device_id_type=MESH),
        pltpu.make_async_remote_copy(
            src_ref=own_n.at[1 - core], dst_ref=came_n, send_sem=pair_sem.at[2], recv_sem=pair_sem.at[3],
            device_id=(mate, y), device_id_type=MESH),
    ]
    for turn, h in enumerate((1 - core, core)):
        lead = h == 0
        vb[h] = vf[h].astype(BF16)
        top = jnp.where(lead, g_top[0:1, :], g_top[1:2, :])
        end = jnp.where(lead, f_end[0:1, :], f_end[1:2, :])
        w = jnp.exp(jnp.where(lead, gcol[:, 0:1], gcol[:, 1:2]) - top)
        kw = kf[h] * w
        state = lax.dot_general(
            kw.astype(BF16), vb[h], (((0,), (0,)), ((), ())), preferred_element_type=F32
        )
        n = jnp.sum(kw, axis=0, keepdims=True)
        own_n[h, 0:1, :] = n[:, :128]
        own_n[h, 1:2, :] = n[:, 128:]
        own_n[h, 2:3, :] = jnp.broadcast_to(end, (1, 128))
        own_n[h, 3:4, :] = jnp.broadcast_to(top + end, (1, 128))
        if turn == 0:
            gone[...] = state.astype(BF16)
            pl.semaphore_wait(barrier, chips + 2)
            for c in swap:
                c.start()
            gather(0, 0)
            gather(1, 0)
        else:
            own_c[...] = state
    for c in swap:
        c.wait()

    mine_n, their_n = own_n[core], came_n[...]
    first = core == 0
    n0, n1 = jnp.where(first, mine_n, their_n), jnp.where(first, their_n, mine_n)
    f0, t0, f1, t1 = n0[2:3], n0[3:4], n1[2:3], n1[3:4]
    top = jnp.maximum(t0 + f1, t1)
    w0, w1 = jnp.exp(t0 + f1 - top), jnp.exp(t1 - top)
    w_mine, w_their = jnp.where(first, w0, w1), jnp.where(first, w1, w0)
    width = own_c.shape[1]
    chip_c[...] = (
        own_c[...] * wide(w_mine, width) + came[...].astype(F32) * wide(w_their, width)
    ).astype(BF16)
    chip_n[0:2, :] = n0[0:2] * w0 + n1[0:2] * w1
    chip_n[2:3, :] = f0 + f1
    chip_n[3:4, :] = top

    def to_owner(other):
        at = pl.ds(pl.multiple_of(other * part, part), part)
        who = (other * 2 + core, y)
        return (
            pltpu.make_async_remote_copy(
                src_ref=chip_n, dst_ref=slots_n.at[chip], send_sem=sns.at[other], recv_sem=rns.at[chip],
                device_id=who, device_id_type=MESH),
            pltpu.make_async_remote_copy(
                src_ref=chip_c.at[at], dst_ref=slots.at[chip], send_sem=ss.at[other], recv_sem=rs.at[chip],
                device_id=who, device_id_type=MESH),
        )

    def from_chip(other):
        who = (other * 2 + core, y)
        return (
            pltpu.make_async_remote_copy(
                src_ref=chip_n, dst_ref=slots_n.at[other], send_sem=sns.at[other], recv_sem=rns.at[other],
                device_id=who, device_id_type=MESH),
            pltpu.make_async_remote_copy(
                src_ref=chip_c.at[pl.ds(0, part)], dst_ref=slots.at[other], send_sem=ss.at[other],
                recv_sem=rs.at[other], device_id=who, device_id_type=MESH),
        )

    def send(i, _):
        for c in to_owner(lax.rem(chip + i, chips)):
            c.start()
        return 0

    lax.fori_loop(1, chips, send, 0)
    gather(0, 1)
    slots_n[chip] = chip_n[...]
    slots[chip] = chip_c[pl.ds(pl.multiple_of(chip * part, part), part), :]

    def attend(h):
        loads[3 * h + 2].wait()
        q = qf[h] * 0.0625
        q_hi = q.astype(BF16)
        q_lo = (q - q_hi.astype(F32)).astype(BF16)
        qf[h] = q
        qc[h, :, 0:256] = q_hi
        qc[h, :, 256:512] = q_hi
        qc[h, :, 512:768] = q_lo
        k = kf[h]
        k_hi = k.astype(BF16)
        k_lo = (k - k_hi.astype(F32)).astype(BF16)
        kc[:, 0:256] = k_hi
        kc[:, 256:512] = k_lo
        kc[:, 512:768] = k_hi
        for i in range(rows // tile):
            at = slice(i * tile, (i + 1) * tile)
            peak_col = gcol[at, 2 + h:3 + h]
            upto = (i + 1) * tile
            s = lax.dot_general(
                qc[h, at, :], kc[0:upto, :], (((1,), (1,)), ((), ())), preferred_element_type=F32
            )
            z = grow[h:h + 1, 0:upto] - peak_col
            r = lax.broadcasted_iota(jnp.int32, (tile, upto), 0) + i * tile
            c = lax.broadcasted_iota(jnp.int32, (tile, upto), 1)
            w = jnp.exp(jnp.where(c <= r, z, -jnp.inf)) * s
            den[h, at, :] = jnp.sum(w, axis=1, keepdims=True)
            num[h, at, :] = jnp.dot(w.astype(BF16), vb[h, 0:upto, :], preferred_element_type=F32)

    for f in range(2, 5):
        gather(f, 0)
    for c in w_loads:
        c.start()
    attend(0)
    gather(1, 1)

    def give_back(other):
        return pltpu.make_async_remote_copy(
            src_ref=back.at[other], dst_ref=prefix.at[pl.ds(pl.multiple_of(chip * part, part), part)],
            send_sem=sb.at[other], recv_sem=rb.at[chip], device_id=(other * 2 + core, y), device_id_type=MESH)

    def take_back(other):
        return pltpu.make_async_remote_copy(
            src_ref=back.at[other], dst_ref=prefix.at[pl.ds(pl.multiple_of(other * part, part), part)],
            send_sem=sb.at[other], recv_sem=rb.at[other], device_id=(other * 2 + core, y), device_id_type=MESH)

    def factors(p, carry):
        m, n = carry

        @pl.when(p != chip)
        def _():
            from_chip(p)[0].wait_recv()

        @pl.when(p == chip)
        def _():
            pre_n[0:2, :] = n
            pre_n[2:3, :] = m

        later = slots_n[p]
        f, t = later[2:3], later[3:4]
        top = jnp.maximum(m + f, t)
        a, b = jnp.exp(m + f - top), jnp.exp(t - top)
        weigh[p, 0:1, :] = a
        weigh[p, 1:2, :] = b
        return top, n * a + later[0:2] * b

    lax.fori_loop(0, chips, factors, (jnp.full((1, 128), LOW, F32), jnp.zeros((2, 128), F32)))

    def scan(p, c):
        @pl.when(p != chip)
        def _():
            from_chip(p)[1].wait_recv()

        back[p] = c.astype(BF16)

        @pl.when(p == chip)
        def _():
            prefix[pl.ds(pl.multiple_of(chip * part, part), part), :] = c.astype(BF16)

        @pl.when(p != chip)
        def _():
            give_back(p).start()

        return c * wide(weigh[p, 0:1, :], width) + slots[p].astype(F32) * wide(weigh[p, 1:2, :], width)

    lax.fori_loop(0, chips, scan, jnp.zeros((part, width), F32))

    attend(1)
    gather(2, 1)

    def got_back(i, _):
        take_back(lax.rem(chip + i, chips)).wait_recv()
        return 0

    lax.fori_loop(1, chips, got_back, 0)

    gather(0, 2)
    pm, pn = pre_n[2:3, :], pre_n[0:2, :]
    top = jnp.maximum(pm + f0, t0)
    a, b = jnp.exp(pm + f0 - top), jnp.exp(t0 - top)
    zero = jnp.zeros_like(b)
    b_mine, b_their = jnp.where(first, b, zero), jnp.where(first, zero, b)
    p_c = prefix[...].astype(F32)
    second_c = (
        p_c * wide(a, width) + own_c[...] * wide(b_mine, width) + came[...].astype(F32) * wide(b_their, width)
    )
    second_n = pn * a + n0[0:2] * b
    fix[core] = jnp.where(first, p_c, second_c).astype(BF16)
    out_c[...] = jnp.where(first, second_c, p_c).astype(BF16)
    fix_n[core, 0:2, :] = jnp.where(first, pn, second_n)
    fix_n[core, 2:3, :] = jnp.where(first, pm, top)
    out_n[0:2, :] = jnp.where(first, second_n, pn)
    out_n[2:3, :] = jnp.where(first, top, pm)
    out_n[3:4, :] = jnp.zeros((1, 128), F32)
    tell = [
        pltpu.make_async_remote_copy(
            src_ref=out_c, dst_ref=fix.at[core], send_sem=pair_sem.at[4], recv_sem=pair_sem.at[5],
            device_id=(mate, y), device_id_type=MESH),
        pltpu.make_async_remote_copy(
            src_ref=out_n, dst_ref=fix_n.at[core], send_sem=pair_sem.at[6], recv_sem=pair_sem.at[7],
            device_id=(mate, y), device_id_type=MESH),
    ]
    for c in tell:
        c.start()

    def finish_head(start, size, h):
        at = pl.ds(pl.multiple_of(start, 32), size)
        pm = fix_n[h, 2:3, 0:1]
        n_row = jnp.concatenate([fix_n[h, 0:1, :], fix_n[h, 1:2, :]], axis=1)
        peak_col = jnp.where(h == 0, gcol[at, 2:3], gcol[at, 3:4])
        top = jnp.maximum(peak_col, pm)
        ow, iw = jnp.exp(peak_col - top), jnp.exp(pm - top)
        mem = jnp.dot(qc[h, at, 0:256], fix[h], preferred_element_type=F32)
        mem_n = jnp.sum(qf[h, at, :] * n_row, axis=1, keepdims=True)
        d = jnp.maximum(jnp.abs(ow * den[h, at, :] + iw * mem_n), 1.0)
        inv = 1.0 / d
        hidden[at, pl.ds(pl.multiple_of(h * width, width), width)] = (
            (ow * inv) * num[h, at, :] + (iw * inv) * mem
        ).astype(BF16)

    def finish(start, size):
        finish_head(start, size, 1 - core)

    def ready_head(i, _):
        finish_head(i * tile, tile, core)
        return 0

    lax.fori_loop(0, rows // tile, ready_head, 0)
    gather(1, 2)
    gather(3, 1)
    for c in tell:
        c.wait()


    edge, small, count = 32, 64, 4
    big = half - edge - small * count

    def rows_at(mine, c):
        base = (kept if mine else 1 - kept) * half + edge
        return base + c * small, (small if c is not count else big)

    def x_copy(c):
        start, size = rows_at(False, c)
        return pltpu.make_async_remote_copy(
            src_ref=hidden.at[pl.ds(pl.multiple_of(start, edge), size)],
            dst_ref=swapped.at[pl.ds(pl.multiple_of(c * small, small), size)], send_sem=xs.at[c], recv_sem=xr.at[c],
            device_id=(ctx, partner), device_id_type=MESH)

    def small_piece(c, p):
        lo, w = ((0, block // 2), (block // 2, block // 2), (0, block))[p]
        return c, p // 2, lo, w, c * 3 + p

    def big_piece(b, j):
        w = block // 4
        return count, b, pl.multiple_of(j * w, w), w, 3 * count + b * 4 + j

    def y_copy(piece):
        c, b, lo, w, i = piece
        at = (b, pl.ds(pl.multiple_of(c * small, small), rows_at(True, c)[1]), pl.ds(lo, w))
        return pltpu.make_async_remote_copy(
            src_ref=y_out.at[at], dst_ref=y_in.at[at], send_sem=ys.at[i], recv_sem=yr.at[i],
            device_id=(ctx, across), device_id_type=MESH)

    def z_copy(piece, incoming):
        c, b, lo, w, i = piece
        start, size = rows_at(not incoming, c)
        return pltpu.make_async_remote_copy(
            src_ref=z_out.at[pl.ds(pl.multiple_of(c * small, small), size), pl.ds(lo, w)],
            dst_ref=out.at[pl.ds(pl.multiple_of(start, edge), size), pl.ds(lo, w)],
            send_sem=zs.at[i], recv_sem=zr.at[i], device_id=(ctx, partner), device_id_type=MESH)

    def project(f, piece):
        c, b, lo, w, i = piece
        start, size = rows_at(True, c)
        return jnp.dot(
            hidden[pl.ds(pl.multiple_of(start, edge), size), :], w_own[f, :, pl.ds(lo, w)],
            preferred_element_type=F32,
        ) + jnp.dot(
            swapped[pl.ds(pl.multiple_of(c * small, small), size), :], w_mate[f, :, pl.ds(lo, w)],
            preferred_element_type=F32,
        )

    def y_step(piece):
        c, b, lo, w, i = piece
        y_out[b, pl.ds(pl.multiple_of(c * small, small), rows_at(True, c)[1]), pl.ds(lo, w)] = project(b, piece).astype(BF16)
        y_copy(piece).start()

    def keep(piece):
        c, b, lo, w, i = piece
        start, size = rows_at(True, c)
        return pltpu.make_async_copy(
            out_own.at[pl.ds(pl.multiple_of(c * small, small), size), pl.ds(lo, w)],
            out.at[pl.ds(pl.multiple_of(start, edge), size), pl.ds(lo, w)], own_sem.at[i])

    def f_step(piece):
        c, b, lo, w, i = piece
        start, size = rows_at(True, c)
        mine = project(2 + b, piece)
        y_copy(piece).wait_recv()
        at = pl.ds(pl.multiple_of(c * small, small), size)
        total = (mine + y_in[b, at, pl.ds(lo, w)].astype(F32)).astype(BF16)
        if b == 0:
            z_out[at, pl.ds(lo, w)] = total
            z_copy(piece, False).start()
        else:
            out_own[at, pl.ds(lo, w)] = total
            keep(piece).start()

    def each(n, body):
        def one(i, _):
            body(i)
            return 0

        lax.fori_loop(0, n, one, 0)

    def finish_chunk(mine, c):
        finish(*rows_at(mine, c))
        if not mine:
            x_copy(c).start()

    ends = (0, half)

    def edge_rows():
        return jnp.concatenate([hidden[pl.ds(e, edge), :] for e in ends], axis=0)

    def edge_copy(b):
        return pltpu.make_async_remote_copy(
            src_ref=e_out.at[b], dst_ref=e_in.at[b], send_sem=edge_s.at[b], recv_sem=edge_r.at[b],
            device_id=(ctx, across), device_id_type=MESH)

    def edge_sum():
        return pltpu.make_async_remote_copy(
            src_ref=e_sum, dst_ref=e_got, send_sem=edge_s.at[2], recv_sem=edge_r.at[2],
            device_id=(ctx, partner), device_id_type=MESH)

    def edge_keep(i):
        return pltpu.make_async_copy(
            e_sum2.at[pl.ds(i * edge, edge)], out.at[pl.ds(ends[i], edge)], edge_k.at[i])

    finish_chunk(False, 0)
    for e in ends:
        finish(e, edge)
    for b in range(2):
        w_loads[b].wait()
        e_out[b] = jnp.dot(edge_rows(), w_own[b], preferred_element_type=F32).astype(BF16)
        edge_copy(b).start()
    finish_chunk(True, 0)
    each(count - 1, lambda i: finish_chunk(False, i + 1))
    finish_chunk(False, count)
    gather(0, 3)
    gather(2, 2)
    gather(4, 1)
    each(count - 1, lambda i: finish_chunk(True, i + 1))
    finish_chunk(True, count)
    w_loads[2].wait()
    w_loads[3].wait()
    gather(1, 3)
    gather(0, 4)

    def first_columns(c):
        x_copy(c).wait_recv()
        y_step(small_piece(c, 0))

        @pl.when(c == 0)
        def _():
            gather(1, 4)
            gather(3, 2)

        y_step(small_piece(c, 1))

        @pl.when(c == 2)
        def _():
            gather(2, 3)
            gather(4, 2)

    each(count, first_columns)
    edge_copy(0).wait_recv()
    e_sum[...] = (
        jnp.dot(edge_rows(), w_own[2], preferred_element_type=F32) + e_in[0].astype(F32)).astype(BF16)
    edge_sum().start()
    gather(2, 4)
    each(count, lambda c: y_step(small_piece(c, 2)))
    gather(3, 3)
    gather(3, 4)

    def for_partner(c):
        f_step(small_piece(c, 0))
        f_step(small_piece(c, 1))

    each(count, for_partner)
    edge_copy(1).wait_recv()
    own_edge = jnp.dot(edge_rows(), w_own[3], preferred_element_type=F32) + e_in[1].astype(F32)
    edge_sum().wait_recv()
    e_sum2[...] = (own_edge + e_got[...].astype(F32)).astype(BF16)
    for i in range(2):
        edge_keep(i).start()
    x_copy(count).wait_recv()
    each(4, lambda j: y_step(big_piece(0, j)))
    each(4, lambda j: y_step(big_piece(1, j)))
    gather(4, 3)
    gather(4, 4)
    each(count, lambda c: f_step(small_piece(c, 2)))
    each(4, lambda j: f_step(big_piece(0, j)))
    each(4, lambda j: f_step(big_piece(1, j)))

    for f in range(5):
        gather_sent(f)
    edge_sum().wait_send()
    for i in range(2):
        edge_copy(i).wait_send()
        edge_keep(i).wait()

    def small_done(c):
        x_copy(c).wait_send()
        keep(small_piece(c, 2)).wait()
        for p in range(3):
            y_copy(small_piece(c, p)).wait_send()
        for p in range(2):
            z_copy(small_piece(c, p), False).wait_send()
            z_copy(small_piece(c, p), True).wait_recv()

    def big_done(j):
        y_copy(big_piece(0, j)).wait_send()
        y_copy(big_piece(1, j)).wait_send()
        keep(big_piece(1, j)).wait()
        z_copy(big_piece(0, j), False).wait_send()
        z_copy(big_piece(0, j), True).wait_recv()

    each(count, small_done)
    x_copy(count).wait_send()
    each(4, big_done)

    def sent(i, _):
        other = lax.rem(chip + i, chips)
        for c in to_owner(other):
            c.wait_send()
        give_back(other).wait_send()
        return 0

    lax.fori_loop(1, chips, sent, 0)


def layer(queries, keys, values, out_weight, gate_in, gate_f):
    rows, heads, dk = queries.shape
    dv = values.shape[2]
    chips = lax.axis_size("ctx") // 2
    part = dk // chips
    hbm = pl.BlockSpec(memory_space=pl.ANY)
    V = pltpu.VMEM
    dma = pltpu.SemaphoreType.DMA
    return pl.pallas_call(
        layer_kernel,
        out_shape=jax.ShapeDtypeStruct((rows, out_weight.shape[1] // 4), BF16),
        in_specs=[hbm] * 6,
        out_specs=hbm,
        scratch_shapes=[
            V((heads, rows), F32), V((heads, rows), F32),
            V((heads, rows, dk), F32), V((heads, rows, dk), F32), V((heads, rows, dv), F32),
            V((heads, rows, 3 * dk), BF16), V((rows, 3 * dk), BF16), V((heads, rows, dv), BF16),
            V((heads, rows, dv), F32), V((heads, rows, 1), F32), V((rows, 8), F32), V((8, rows), F32),
            V((dk, dv), F32), V((heads, 4, 128), F32), V((dk, dv), BF16), V((4, 128), F32),
            V((dk, dv), BF16), V((4, 128), F32),
            V((dk, dv), BF16), V((4, 128), F32), V((chips, part, dv), BF16), V((chips, 4, 128), F32),
            V((chips, part, dv), BF16), V((dk, dv), BF16), V((4, 128), F32),
            V((heads, dk, dv), BF16), V((heads, 4, 128), F32), V((dk, dv), BF16), V((4, 128), F32),
            V((rows, heads * dv), BF16), V((rows // 2, heads * dv), BF16),
            V((4, heads * dv, out_weight.shape[1] // 4), BF16), V((4, heads * dv, out_weight.shape[1] // 4), BF16),
            V((2, rows // 2, out_weight.shape[1] // 4), BF16), V((2, rows // 2, out_weight.shape[1] // 4), BF16),
            V((rows // 2, out_weight.shape[1] // 4), BF16),
            V((chips, 2, 128), F32),
            V((2, 64, out_weight.shape[1] // 4), BF16), V((2, 64, out_weight.shape[1] // 4), BF16),
            V((64, out_weight.shape[1] // 4), BF16), V((64, out_weight.shape[1] // 4), BF16),
            V((64, out_weight.shape[1] // 4), BF16), dma((3,)), dma((3,)), dma((2,)),
            V((rows // 2, out_weight.shape[1] // 4), BF16), dma((2,)), dma((20,)), dma((2, 3)), dma((4,)), dma((8,)), dma((chips,)), dma((chips,)), dma((chips,)), dma((chips,)),
            dma((chips,)), dma((chips,)),
            dma((5, 2)), dma((5, 2)), dma((5, 2, 6)), dma((5, 2, 6)), dma((5,)), dma((5,)),
            dma((5,)), dma((5,)), dma((20,)), dma((20,)), dma((20,)), dma((20,)),
        ],
        compiler_params=pltpu.CompilerParams(
            collective_id=0, has_side_effects=True, vmem_limit_bytes=60 << 20
        ),
        name="layer",
    )(queries, keys, values, out_weight, gate_in, gate_f)


def hand_kernel(src, dst, held, in_sem, out_sem):
    count = in_sem.shape[0]
    size = src.shape[0] // count
    at = [pl.ds(i * size, size) for i in range(count)]
    take = [pltpu.make_async_copy(src.at[a], held.at[a], in_sem.at[i]) for i, a in enumerate(at)]
    give = [pltpu.make_async_copy(held.at[a], dst.at[a], out_sem.at[i]) for i, a in enumerate(at)]
    for c in take:
        c.start()
    for c, d in zip(take, give):
        c.wait()
        d.start()
    for d in give:
        d.wait()


def handed_on(x):
    hbm = pl.BlockSpec(memory_space=pl.ANY)
    return pl.pallas_call(
        hand_kernel,
        out_shape=jax.ShapeDtypeStruct(x.shape, x.dtype),
        in_specs=[hbm],
        out_specs=hbm,
        scratch_shapes=[pltpu.VMEM(x.shape, x.dtype), pltpu.SemaphoreType.DMA((8,)), pltpu.SemaphoreType.DMA((8,))],
        name="hand_on",
    )(x)


def on_device(queries, keys, values, entry_gate_logit, forget_gate, out_weight):
    return handed_on(layer(queries, keys, values, out_weight, entry_gate_logit, forget_gate))


def solution(mesh):
    placed = (
        P("ctx", "head", None),
        P("ctx", "head", None),
        P("ctx", "head", None),
        P("head", "ctx"),
        P("head", "ctx"),
        P("head", None),
    )
    return jax.shard_map(
        on_device, mesh=mesh, in_specs=placed, out_specs=P("ctx", "head"), check_vma=False
    )
```

```python
import functools

import jax
import jax.numpy as jnp
from jax import lax
from jax.experimental import pallas as pl
from jax.experimental.pallas import tpu as pltpu
from jax.sharding import PartitionSpec as P

MESH = pl.DeviceIdType.MESH
F32, BF16 = jnp.float32, jnp.bfloat16
LOW = -1e30


def running(x, join, fill):
    lane = lax.broadcasted_iota(jnp.int32, x.shape, 1)
    row = lax.broadcasted_iota(jnp.int32, x.shape, 0)
    for step in (1, 2, 4, 8, 16, 32, 64):
        x = join(x, jnp.where(lane >= step, pltpu.roll(x, step, 1), fill))
    ends = jnp.broadcast_to(x[:, 127:128], x.shape)
    ends = jnp.where(row >= 2, pltpu.roll(ends, 2, 0), fill)
    for step in (2, 4, 8):
        ends = join(ends, jnp.where(row >= step, pltpu.roll(ends, step, 0), fill))
    return join(x, ends)


def stacked(x):
    return jnp.concatenate([x[:, j:j + 128] for j in range(0, x.shape[1], 128)], axis=0)


def unstacked(x):
    return jnp.concatenate([x[j:j + 2, :] for j in range(0, x.shape[0], 2)], axis=1)


def log_sigmoid(x):
    e = jnp.exp(-jnp.abs(x))
    u = 1.0 + e
    tail = jnp.where(u == 1.0, e, jnp.log(u) * (e / jnp.where(u == 1.0, 1.0, u - 1.0)))
    return jnp.minimum(x, 0.0) - tail


def wide(row, width):
    return jnp.concatenate([row] * (width // row.shape[1]), axis=1)


def layer_kernel(
    q_hbm, k_hbm, v_hbm, w_hbm, in_hbm, f_hbm, out,
    gate_in, gate_f,
    qf, kf, vf, qc, kc, vb, num, den, gcol, grow, own_c, own_n, gone, gone_n, came, came_n,
    chip_c, chip_n, slots, slots_n, back, prefix, pre_n, fix, fix_n, out_c, out_n,
    hidden, swapped, w_own, w_mate, y_out, y_in, z_out,
    plane_sem, weigh, e_out, e_in, e_sum, e_got, e_sum2, edge_s, edge_r, edge_k, out_own, gate_sem, own_sem, load_sem, w_sem, pair_sem, ss, rs, sns, rns, sb, rb,
    fetch_s, fetch_r, ring_s, ring_r, share_s, share_r, xs, xr, ys, yr, zs, zr,
):
    rows = q_hbm.shape[0]
    tile = 256
    ctx, y = lax.axis_index("ctx"), lax.axis_index("head")
    core = lax.rem(ctx, 2)
    chip = lax.div(ctx, 2)
    mate = ctx + 1 - 2 * core
    chips = slots.shape[0]
    part = slots.shape[1]
    side = lax.rem(y, 2)
    pair = lax.div(y, 2)
    partner = y + 1 - 2 * side
    across = 3 - y
    kept = lax.rem(lax.div(y + 1, 2), 2)
    cx, cz = lax.rem(chip, 4), lax.div(chip, 4)
    half = rows // 2
    block = w_own.shape[2]

    def column(b, part_of, of_y):
        other = of_y + 1 - 2 * part_of
        start = (lax.div(of_y, 2) * -2 + 2 + part_of, lax.div(of_y, 2) * -2 + 3 - part_of, other, of_y)[b]
        return start * block

    barrier = pltpu.get_barrier_semaphore()
    for who in ((mate, y), (ctx, partner), (ctx, across)):
        pl.semaphore_signal(barrier, inc=1, device_id=who, device_id_type=MESH)

    x_line = [(cz * 4 + lax.rem(cx + i, 4)) * 2 + core for i in range(1, 4)]
    z_line = [(lax.rem(cz + i, 4) * 4 + cx) * 2 + core for i in range(1, 4)]
    for other in x_line + z_line:
        pl.semaphore_signal(barrier, inc=1, device_id=(other, y), device_id_type=MESH)

    gates = [
        pltpu.make_async_copy(f_hbm, gate_f, gate_sem.at[0]),
        pltpu.make_async_copy(in_hbm, gate_in, gate_sem.at[1]),
    ]
    for c in gates:
        c.start()
    loads = []
    for h in range(2):
        for j, (src, dst) in enumerate(((k_hbm, kf), (v_hbm, vf), (q_hbm, qf))):
            loads.append(pltpu.make_async_copy(src.at[:, h, :], dst.at[h], load_sem.at[h, j]))
    for c in (0, 1, 3, 4, 2, 5):
        loads[c].start()
    w_loads = [
        pltpu.make_async_copy(
            w_hbm.at[:, pl.ds(pl.multiple_of(column(b, side, y), block), block)], w_own.at[b], w_sem.at[b])
        for b in range(4)
    ]

    parts = ((0, 0, block // 2), (0, block // 2, block // 2), (1, 0, block), (2, 0, block), (3, 0, block))

    def strip(f, path, z_at, x_at, count):
        at = z_at * 4 + x_at if path == 0 else x_at * 4 + z_at
        b, lo, width = parts[f]
        return w_mate.at[
            b, pl.ds(pl.multiple_of((core * 2 + path) * 256 + at * 16, 16), 16 * count), pl.ds(lo, width)]

    def fetch(f, path):
        at = cz * 4 + cx if path == 0 else cx * 4 + cz
        b, lo, width = parts[f]
        col = column(b, 1 - side, partner) + lo
        return pltpu.make_async_remote_copy(
            src_ref=w_hbm.at[
                pl.ds(pl.multiple_of((core * 2 + path) * 256 + at * 16, 16), 16),
                pl.ds(pl.multiple_of(col, 128), width)],
            dst_ref=strip(f, path, cz, cx, 1),
            send_sem=fetch_s.at[f, path], recv_sem=fetch_r.at[f, path], device_id=(ctx, partner), device_id_type=MESH)

    def spread(f, path, stage, way, incoming):
        along_x = (path == 0) == (stage == 0)
        here = cx if along_x else cz
        to = lax.rem(here + way, 4)
        owner = lax.rem(here + 4 - way, 4) if incoming else here
        if stage == 0:
            ref = strip(f, path, cz, owner, 1) if along_x else strip(f, path, owner, cx, 1)
        else:
            ref = strip(f, path, 0, owner, 4) if along_x else strip(f, path, owner, 0, 4)
        peer = (cz * 4 + to if along_x else to * 4 + cx) * 2 + core
        i = stage * 3 + way - 1
        return pltpu.make_async_remote_copy(
            src_ref=ref, dst_ref=ref, send_sem=ring_s.at[f, path, i], recv_sem=ring_r.at[f, path, i],
            device_id=(peer, y), device_id_type=MESH)

    def share(f, who):
        b, lo, width = parts[f]
        ref = w_mate.at[b, pl.ds(pl.multiple_of(who * 512, 512), 512), pl.ds(lo, width)]
        return pltpu.make_async_remote_copy(
            src_ref=ref, dst_ref=ref, send_sem=share_s.at[f], recv_sem=share_r.at[f],
            device_id=(mate, y), device_id_type=MESH)

    def gather(f, *steps):
        for step in steps:
            for path in range(2):
                if step == 0:
                    fetch(f, path).start()
                if step == 1:
                    fetch(f, path).wait_recv()
                for way in (1, 3, 2):
                    if step == 2 or step == 3:
                        spread(f, path, step - 2, way, True).wait_recv()
                for way in (1, 3, 2):
                    if step == 1 or step == 2:
                        spread(f, path, step - 1, way, False).start()
            if step == 3:
                share(f, core).start()
            if step == 4:
                share(f, 1 - core).wait_recv()

    def gather_sent(f):
        for path in range(2):
            fetch(f, path).wait_send()
            for i in range(6):
                spread(f, path, i // 3, i % 3 + 1, False).wait_send()
        share(f, core).wait_send()

    for c in gates:
        c.wait()
    cum = running(log_sigmoid(stacked(gate_f[...])), jnp.add, 0.0)
    g = stacked(gate_in[...]) - cum
    peak = running(g, jnp.maximum, LOW)
    f_end = cum[14:16, 127:128]
    g_top = peak[14:16, 127:128]
    g, peak = unstacked(g), unstacked(peak)
    grow[0:2, :] = g
    gcol[...] = jnp.transpose(jnp.concatenate([g, peak, g, peak], axis=0), (1, 0))
    for c in (0, 1, 3, 4):
        loads[c].wait()
    swap = [
        pltpu.make_async_remote_copy(
            src_ref=gone, dst_ref=came, send_sem=pair_sem.at[0], recv_sem=pair_sem.at[1],
            device_id=(mate, y), device_id_type=MESH),
        pltpu.make_async_remote_copy(
            src_ref=own_n.at[1 - core], dst_ref=came_n, send_sem=pair_sem.at[2], recv_sem=pair_sem.at[3],
            device_id=(mate, y), device_id_type=MESH),
    ]
    for turn, h in enumerate((1 - core, core)):
        lead = h == 0
        vb[h] = vf[h].astype(BF16)
        top = jnp.where(lead, g_top[0:1, :], g_top[1:2, :])
        end = jnp.where(lead, f_end[0:1, :], f_end[1:2, :])
        w = jnp.exp(jnp.where(lead, gcol[:, 0:1], gcol[:, 1:2]) - top)
        kw = kf[h] * w
        state = lax.dot_general(
            kw.astype(BF16), vb[h], (((0,), (0,)), ((), ())), preferred_element_type=F32
        )
        n = jnp.sum(kw, axis=0, keepdims=True)
        own_n[h, 0:1, :] = n[:, :128]
        own_n[h, 1:2, :] = n[:, 128:]
        own_n[h, 2:3, :] = jnp.broadcast_to(end, (1, 128))
        own_n[h, 3:4, :] = jnp.broadcast_to(top + end, (1, 128))
        if turn == 0:
            gone[...] = state.astype(BF16)
            pl.semaphore_wait(barrier, 9)
            for other in z_line:
                pl.semaphore_signal(plane_sem, inc=1, device_id=(other, y), device_id_type=MESH)
            for c in swap:
                c.start()
            gather(0, 0)
            gather(1, 0)
        else:
            own_c[...] = state
    for c in swap:
        c.wait()

    mine_n, their_n = own_n[core], came_n[...]
    first = core == 0
    n0, n1 = jnp.where(first, mine_n, their_n), jnp.where(first, their_n, mine_n)
    f0, t0, f1, t1 = n0[2:3], n0[3:4], n1[2:3], n1[3:4]
    top = jnp.maximum(t0 + f1, t1)
    w0, w1 = jnp.exp(t0 + f1 - top), jnp.exp(t1 - top)
    w_mine, w_their = jnp.where(first, w0, w1), jnp.where(first, w1, w0)
    width = own_c.shape[1]
    chip_c[...] = (
        own_c[...] * wide(w_mine, width) + came[...].astype(F32) * wide(w_their, width)
    ).astype(BF16)
    chip_n[0:2, :] = n0[0:2] * w0 + n1[0:2] * w1
    chip_n[2:3, :] = f0 + f1
    chip_n[3:4, :] = top

    def to_owner(other):
        at = pl.ds(pl.multiple_of(other * part, part), part)
        who = (other * 2 + core, y)
        return (
            pltpu.make_async_remote_copy(
                src_ref=chip_n, dst_ref=slots_n.at[chip], send_sem=sns.at[other], recv_sem=rns.at[chip],
                device_id=who, device_id_type=MESH),
            pltpu.make_async_remote_copy(
                src_ref=chip_c.at[at], dst_ref=slots.at[chip], send_sem=ss.at[other], recv_sem=rs.at[chip],
                device_id=who, device_id_type=MESH),
        )

    def from_chip(other):
        who = (other * 2 + core, y)
        return (
            pltpu.make_async_remote_copy(
                src_ref=chip_n, dst_ref=slots_n.at[other], send_sem=sns.at[other], recv_sem=rns.at[other],
                device_id=who, device_id_type=MESH),
            pltpu.make_async_remote_copy(
                src_ref=chip_c.at[pl.ds(0, part)], dst_ref=slots.at[other], send_sem=ss.at[other],
                recv_sem=rs.at[other], device_id=who, device_id_type=MESH),
        )

    def send(i, _):
        for c in to_owner(lax.rem(chip + i, chips)):
            c.start()
        return 0

    pl.semaphore_wait(plane_sem, 3)
    lax.fori_loop(1, chips, send, 0)
    gather(0, 1)
    slots_n[chip] = chip_n[...]
    slots[chip] = chip_c[pl.ds(pl.multiple_of(chip * part, part), part), :]

    def attend(h):
        loads[3 * h + 2].wait()
        q = qf[h] * 0.0625
        q_hi = q.astype(BF16)
        q_lo = (q - q_hi.astype(F32)).astype(BF16)
        qf[h] = q
        qc[h, :, 0:256] = q_hi
        qc[h, :, 256:512] = q_hi
        qc[h, :, 512:768] = q_lo
        k = kf[h]
        k_hi = k.astype(BF16)
        k_lo = (k - k_hi.astype(F32)).astype(BF16)
        kc[:, 0:256] = k_hi
        kc[:, 256:512] = k_lo
        kc[:, 512:768] = k_hi
        for i in range(rows // tile):
            at = slice(i * tile, (i + 1) * tile)
            peak_col = gcol[at, 2 + h:3 + h]
            upto = (i + 1) * tile
            s = lax.dot_general(
                qc[h, at, :], kc[0:upto, :], (((1,), (1,)), ((), ())), preferred_element_type=F32
            )
            z = grow[h:h + 1, 0:upto] - peak_col
            r = lax.broadcasted_iota(jnp.int32, (tile, upto), 0) + i * tile
            c = lax.broadcasted_iota(jnp.int32, (tile, upto), 1)
            w = jnp.exp(jnp.where(c <= r, z, -jnp.inf)) * s
            den[h, at, :] = jnp.sum(w, axis=1, keepdims=True)
            num[h, at, :] = jnp.dot(w.astype(BF16), vb[h, 0:upto, :], preferred_element_type=F32)

    for f in range(2, 5):
        gather(f, 0)
    for c in w_loads:
        c.start()
    attend(0)
    gather(1, 1)

    def give_back(other):
        return pltpu.make_async_remote_copy(
            src_ref=back.at[other], dst_ref=prefix.at[pl.ds(pl.multiple_of(chip * part, part), part)],
            send_sem=sb.at[other], recv_sem=rb.at[chip], device_id=(other * 2 + core, y), device_id_type=MESH)

    def take_back(other):
        return pltpu.make_async_remote_copy(
            src_ref=back.at[other], dst_ref=prefix.at[pl.ds(pl.multiple_of(other * part, part), part)],
            send_sem=sb.at[other], recv_sem=rb.at[other], device_id=(other * 2 + core, y), device_id_type=MESH)

    def factors(p, carry):
        m, n = carry

        @pl.when(p != chip)
        def _():
            from_chip(p)[0].wait_recv()

        @pl.when(p == chip)
        def _():
            pre_n[0:2, :] = n
            pre_n[2:3, :] = m

        later = slots_n[p]
        f, t = later[2:3], later[3:4]
        top = jnp.maximum(m + f, t)
        a, b = jnp.exp(m + f - top), jnp.exp(t - top)
        weigh[p, 0:1, :] = a
        weigh[p, 1:2, :] = b
        return top, n * a + later[0:2] * b

    lax.fori_loop(0, chips, factors, (jnp.full((1, 128), LOW, F32), jnp.zeros((2, 128), F32)))

    def scan(p, c):
        @pl.when(p != chip)
        def _():
            from_chip(p)[1].wait_recv()

        back[p] = c.astype(BF16)

        @pl.when(p == chip)
        def _():
            prefix[pl.ds(pl.multiple_of(chip * part, part), part), :] = c.astype(BF16)

        @pl.when(p != chip)
        def _():
            give_back(p).start()

        return c * wide(weigh[p, 0:1, :], width) + slots[p].astype(F32) * wide(weigh[p, 1:2, :], width)

    lax.fori_loop(0, chips, scan, jnp.zeros((part, width), F32))

    attend(1)
    gather(2, 1)

    def got_back(i, _):
        take_back(lax.rem(chip + i, chips)).wait_recv()
        return 0

    lax.fori_loop(1, chips, got_back, 0)

    gather(0, 2)
    pm, pn = pre_n[2:3, :], pre_n[0:2, :]
    top = jnp.maximum(pm + f0, t0)
    a, b = jnp.exp(pm + f0 - top), jnp.exp(t0 - top)
    zero = jnp.zeros_like(b)
    b_mine, b_their = jnp.where(first, b, zero), jnp.where(first, zero, b)
    p_c = prefix[...].astype(F32)
    second_c = (
        p_c * wide(a, width) + own_c[...] * wide(b_mine, width) + came[...].astype(F32) * wide(b_their, width)
    )
    second_n = pn * a + n0[0:2] * b
    fix[core] = jnp.where(first, p_c, second_c).astype(BF16)
    out_c[...] = jnp.where(first, second_c, p_c).astype(BF16)
    fix_n[core, 0:2, :] = jnp.where(first, pn, second_n)
    fix_n[core, 2:3, :] = jnp.where(first, pm, top)
    out_n[0:2, :] = jnp.where(first, second_n, pn)
    out_n[2:3, :] = jnp.where(first, top, pm)
    out_n[3:4, :] = jnp.zeros((1, 128), F32)
    tell = [
        pltpu.make_async_remote_copy(
            src_ref=out_c, dst_ref=fix.at[core], send_sem=pair_sem.at[4], recv_sem=pair_sem.at[5],
            device_id=(mate, y), device_id_type=MESH),
        pltpu.make_async_remote_copy(
            src_ref=out_n, dst_ref=fix_n.at[core], send_sem=pair_sem.at[6], recv_sem=pair_sem.at[7],
            device_id=(mate, y), device_id_type=MESH),
    ]
    for c in tell:
        c.start()

    def finish_head(start, size, h):
        at = pl.ds(pl.multiple_of(start, 32), size)
        pm = fix_n[h, 2:3, 0:1]
        n_row = jnp.concatenate([fix_n[h, 0:1, :], fix_n[h, 1:2, :]], axis=1)
        peak_col = jnp.where(h == 0, gcol[at, 2:3], gcol[at, 3:4])
        top = jnp.maximum(peak_col, pm)
        ow, iw = jnp.exp(peak_col - top), jnp.exp(pm - top)
        mem = jnp.dot(qc[h, at, 0:256], fix[h], preferred_element_type=F32)
        mem_n = jnp.sum(qf[h, at, :] * n_row, axis=1, keepdims=True)
        d = jnp.maximum(jnp.abs(ow * den[h, at, :] + iw * mem_n), 1.0)
        inv = 1.0 / d
        hidden[at, pl.ds(pl.multiple_of(h * width, width), width)] = (
            (ow * inv) * num[h, at, :] + (iw * inv) * mem
        ).astype(BF16)

    def finish(start, size):
        finish_head(start, size, 1 - core)

    def ready_head(i, _):
        finish_head(i * tile, tile, core)
        return 0

    lax.fori_loop(0, rows // tile, ready_head, 0)
    gather(1, 2)
    gather(3, 1)
    for c in tell:
        c.wait()


    edge, small, count = 32, 64, 4
    big = half - edge - small * count

    def rows_at(mine, c):
        base = (kept if mine else 1 - kept) * half + edge
        return base + c * small, (small if c is not count else big)

    def x_copy(c):
        start, size = rows_at(False, c)
        return pltpu.make_async_remote_copy(
            src_ref=hidden.at[pl.ds(pl.multiple_of(start, edge), size)],
            dst_ref=swapped.at[pl.ds(pl.multiple_of(c * small, small), size)], send_sem=xs.at[c], recv_sem=xr.at[c],
            device_id=(ctx, partner), device_id_type=MESH)

    def small_piece(c, p):
        lo, w = ((0, block // 2), (block // 2, block // 2), (0, block))[p]
        return c, p // 2, lo, w, c * 3 + p

    def big_piece(b, j):
        w = block // 4
        return count, b, pl.multiple_of(j * w, w), w, 3 * count + b * 4 + j

    def y_copy(piece):
        c, b, lo, w, i = piece
        at = (b, pl.ds(pl.multiple_of(c * small, small), rows_at(True, c)[1]), pl.ds(lo, w))
        return pltpu.make_async_remote_copy(
            src_ref=y_out.at[at], dst_ref=y_in.at[at], send_sem=ys.at[i], recv_sem=yr.at[i],
            device_id=(ctx, across), device_id_type=MESH)

    def z_copy(piece, incoming):
        c, b, lo, w, i = piece
        start, size = rows_at(not incoming, c)
        return pltpu.make_async_remote_copy(
            src_ref=z_out.at[pl.ds(pl.multiple_of(c * small, small), size), pl.ds(lo, w)],
            dst_ref=out.at[pl.ds(pl.multiple_of(start, edge), size), pl.ds(lo, w)],
            send_sem=zs.at[i], recv_sem=zr.at[i], device_id=(ctx, partner), device_id_type=MESH)

    def project(f, piece):
        c, b, lo, w, i = piece
        start, size = rows_at(True, c)
        return jnp.dot(
            hidden[pl.ds(pl.multiple_of(start, edge), size), :], w_own[f, :, pl.ds(lo, w)],
            preferred_element_type=F32,
        ) + jnp.dot(
            swapped[pl.ds(pl.multiple_of(c * small, small), size), :], w_mate[f, :, pl.ds(lo, w)],
            preferred_element_type=F32,
        )

    def y_step(piece):
        c, b, lo, w, i = piece
        y_out[b, pl.ds(pl.multiple_of(c * small, small), rows_at(True, c)[1]), pl.ds(lo, w)] = project(b, piece).astype(BF16)
        y_copy(piece).start()

    def keep(piece):
        c, b, lo, w, i = piece
        start, size = rows_at(True, c)
        return pltpu.make_async_copy(
            out_own.at[pl.ds(pl.multiple_of(c * small, small), size), pl.ds(lo, w)],
            out.at[pl.ds(pl.multiple_of(start, edge), size), pl.ds(lo, w)], own_sem.at[i])

    def f_step(piece):
        c, b, lo, w, i = piece
        start, size = rows_at(True, c)
        mine = project(2 + b, piece)
        y_copy(piece).wait_recv()
        at = pl.ds(pl.multiple_of(c * small, small), size)
        total = (mine + y_in[b, at, pl.ds(lo, w)].astype(F32)).astype(BF16)
        if b == 0:
            z_out[at, pl.ds(lo, w)] = total
            z_copy(piece, False).start()
        else:
            out_own[at, pl.ds(lo, w)] = total
            keep(piece).start()

    def each(n, body):
        def one(i, _):
            body(i)
            return 0

        lax.fori_loop(0, n, one, 0)

    def finish_chunk(mine, c):
        finish(*rows_at(mine, c))
        if not mine:
            x_copy(c).start()

    ends = (0, half)

    def edge_rows():
        return jnp.concatenate([hidden[pl.ds(e, edge), :] for e in ends], axis=0)

    def edge_copy(b):
        return pltpu.make_async_remote_copy(
            src_ref=e_out.at[b], dst_ref=e_in.at[b], send_sem=edge_s.at[b], recv_sem=edge_r.at[b],
            device_id=(ctx, across), device_id_type=MESH)

    def edge_sum():
        return pltpu.make_async_remote_copy(
            src_ref=e_sum, dst_ref=e_got, send_sem=edge_s.at[2], recv_sem=edge_r.at[2],
            device_id=(ctx, partner), device_id_type=MESH)

    def edge_keep(i):
        return pltpu.make_async_copy(
            e_sum2.at[pl.ds(i * edge, edge)], out.at[pl.ds(ends[i], edge)], edge_k.at[i])

    finish_chunk(False, 0)
    for e in ends:
        finish(e, edge)
    for b in range(2):
        w_loads[b].wait()
        e_out[b] = jnp.dot(edge_rows(), w_own[b], preferred_element_type=F32).astype(BF16)
        edge_copy(b).start()
    finish_chunk(True, 0)
    each(count - 1, lambda i: finish_chunk(False, i + 1))
    finish_chunk(False, count)
    gather(0, 3)
    gather(2, 2)
    gather(4, 1)
    each(count - 1, lambda i: finish_chunk(True, i + 1))
    finish_chunk(True, count)
    w_loads[2].wait()
    w_loads[3].wait()
    gather(1, 3)
    gather(0, 4)

    def first_columns(c):
        x_copy(c).wait_recv()
        y_step(small_piece(c, 0))

        @pl.when(c == 0)
        def _():
            gather(1, 4)
            gather(3, 2)

        y_step(small_piece(c, 1))

        @pl.when(c == 2)
        def _():
            gather(2, 3)
            gather(4, 2)

    each(count, first_columns)
    edge_copy(0).wait_recv()
    e_sum[...] = (
        jnp.dot(edge_rows(), w_own[2], preferred_element_type=F32) + e_in[0].astype(F32)).astype(BF16)
    edge_sum().start()
    gather(2, 4)
    each(count, lambda c: y_step(small_piece(c, 2)))
    gather(3, 3)
    gather(3, 4)

    def for_partner(c):
        f_step(small_piece(c, 0))
        f_step(small_piece(c, 1))

    each(count, for_partner)
    edge_copy(1).wait_recv()
    own_edge = jnp.dot(edge_rows(), w_own[3], preferred_element_type=F32) + e_in[1].astype(F32)
    edge_sum().wait_recv()
    e_sum2[...] = (own_edge + e_got[...].astype(F32)).astype(BF16)
    for i in range(2):
        edge_keep(i).start()
    x_copy(count).wait_recv()
    each(4, lambda j: y_step(big_piece(0, j)))
    each(4, lambda j: y_step(big_piece(1, j)))
    gather(4, 3)
    gather(4, 4)
    each(count, lambda c: f_step(small_piece(c, 2)))
    each(4, lambda j: f_step(big_piece(0, j)))
    each(4, lambda j: f_step(big_piece(1, j)))

    for f in range(5):
        gather_sent(f)
    edge_sum().wait_send()
    for i in range(2):
        edge_copy(i).wait_send()
        edge_keep(i).wait()

    def small_done(c):
        x_copy(c).wait_send()
        keep(small_piece(c, 2)).wait()
        for p in range(3):
            y_copy(small_piece(c, p)).wait_send()
        for p in range(2):
            z_copy(small_piece(c, p), False).wait_send()
            z_copy(small_piece(c, p), True).wait_recv()

    def big_done(j):
        y_copy(big_piece(0, j)).wait_send()
        y_copy(big_piece(1, j)).wait_send()
        keep(big_piece(1, j)).wait()
        z_copy(big_piece(0, j), False).wait_send()
        z_copy(big_piece(0, j), True).wait_recv()

    each(count, small_done)
    x_copy(count).wait_send()
    each(4, big_done)

    def sent(i, _):
        other = lax.rem(chip + i, chips)
        for c in to_owner(other):
            c.wait_send()
        give_back(other).wait_send()
        return 0

    lax.fori_loop(1, chips, sent, 0)


def layer(queries, keys, values, out_weight, gate_in, gate_f):
    rows, heads, dk = queries.shape
    dv = values.shape[2]
    chips = lax.axis_size("ctx") // 2
    part = dk // chips
    hbm = pl.BlockSpec(memory_space=pl.ANY)
    V = pltpu.VMEM
    dma = pltpu.SemaphoreType.DMA
    return pl.pallas_call(
        layer_kernel,
        out_shape=jax.ShapeDtypeStruct((rows, out_weight.shape[1] // 4), BF16),
        in_specs=[hbm] * 6,
        out_specs=hbm,
        scratch_shapes=[
            V((heads, rows), F32), V((heads, rows), F32),
            V((heads, rows, dk), F32), V((heads, rows, dk), F32), V((heads, rows, dv), F32),
            V((heads, rows, 3 * dk), BF16), V((rows, 3 * dk), BF16), V((heads, rows, dv), BF16),
            V((heads, rows, dv), F32), V((heads, rows, 1), F32), V((rows, 8), F32), V((8, rows), F32),
            V((dk, dv), F32), V((heads, 4, 128), F32), V((dk, dv), BF16), V((4, 128), F32),
            V((dk, dv), BF16), V((4, 128), F32),
            V((dk, dv), BF16), V((4, 128), F32), V((chips, part, dv), BF16), V((chips, 4, 128), F32),
            V((chips, part, dv), BF16), V((dk, dv), BF16), V((4, 128), F32),
            V((heads, dk, dv), BF16), V((heads, 4, 128), F32), V((dk, dv), BF16), V((4, 128), F32),
            V((rows, heads * dv), BF16), V((rows // 2, heads * dv), BF16),
            V((4, heads * dv, out_weight.shape[1] // 4), BF16), V((4, heads * dv, out_weight.shape[1] // 4), BF16),
            V((2, rows // 2, out_weight.shape[1] // 4), BF16), V((2, rows // 2, out_weight.shape[1] // 4), BF16),
            V((rows // 2, out_weight.shape[1] // 4), BF16),
            pltpu.SemaphoreType.REGULAR, V((chips, 2, 128), F32),
            V((2, 64, out_weight.shape[1] // 4), BF16), V((2, 64, out_weight.shape[1] // 4), BF16),
            V((64, out_weight.shape[1] // 4), BF16), V((64, out_weight.shape[1] // 4), BF16),
            V((64, out_weight.shape[1] // 4), BF16), dma((3,)), dma((3,)), dma((2,)),
            V((rows // 2, out_weight.shape[1] // 4), BF16), dma((2,)), dma((20,)), dma((2, 3)), dma((4,)), dma((8,)), dma((chips,)), dma((chips,)), dma((chips,)), dma((chips,)),
            dma((chips,)), dma((chips,)),
            dma((5, 2)), dma((5, 2)), dma((5, 2, 6)), dma((5, 2, 6)), dma((5,)), dma((5,)),
            dma((5,)), dma((5,)), dma((20,)), dma((20,)), dma((20,)), dma((20,)),
        ],
        compiler_params=pltpu.CompilerParams(
            collective_id=0, has_side_effects=True, vmem_limit_bytes=60 << 20
        ),
        name="layer",
    )(queries, keys, values, out_weight, gate_in, gate_f)


def hand_kernel(src, dst, held, in_sem, out_sem):
    count = in_sem.shape[0]
    size = src.shape[0] // count
    at = [pl.ds(i * size, size) for i in range(count)]
    take = [pltpu.make_async_copy(src.at[a], held.at[a], in_sem.at[i]) for i, a in enumerate(at)]
    give = [pltpu.make_async_copy(held.at[a], dst.at[a], out_sem.at[i]) for i, a in enumerate(at)]
    for c in take:
        c.start()
    for c, d in zip(take, give):
        c.wait()
        d.start()
    for d in give:
        d.wait()


def handed_on(x):
    hbm = pl.BlockSpec(memory_space=pl.ANY)
    return pl.pallas_call(
        hand_kernel,
        out_shape=jax.ShapeDtypeStruct(x.shape, x.dtype),
        in_specs=[hbm],
        out_specs=hbm,
        scratch_shapes=[pltpu.VMEM(x.shape, x.dtype), pltpu.SemaphoreType.DMA((4,)), pltpu.SemaphoreType.DMA((4,))],
        name="hand_on",
    )(x)


def on_device(queries, keys, values, entry_gate_logit, forget_gate, out_weight):
    return handed_on(layer(queries, keys, values, out_weight, entry_gate_logit, forget_gate))


def solution(mesh):
    placed = (
        P("ctx", "head", None),
        P("ctx", "head", None),
        P("ctx", "head", None),
        P("head", "ctx"),
        P("head", "ctx"),
        P("head", None),
    )
    return jax.shard_map(
        on_device, mesh=mesh, in_specs=placed, out_specs=P("ctx", "head"), check_vma=False
    )
```
